128 devices in a mesh: section: 8 (over z_hi, x), peer: 16 (over z_lo, y, core).
Axes of the slice: x: 4, y: 4, z: 4 (z_hi: 2, z_lo: 2; z = z_hi * 2 + z_lo), core: 2. Of those that a mesh axis runs over, the one named last changes fastest.
Arguments:
- acts: bfloat16 [4096, 5120], P('section', 'peer'), may hold values from -50 to 50
- grad_out: bfloat16 [4096, 5120], P('section', 'peer'), may hold values from -6 to 6
- gain: bfloat16 [8, 5120], P('section', 'peer'), may hold values from 0.099609375 to 1.8984375
- w_up: bfloat16 [8, 5120, 10240], P('section', None, 'peer'), may hold values from -0.078125 to 0.078125
- w_down: bfloat16 [8, 10240, 5120], P('section', 'peer'), may hold values from -0.0625 to 0.0625
- senders: int32 [128, 1], replicated, may hold values from 0 to 15; in each aligned block of 16 rows (0 to 15, 16 to 31, ...) at most 2 rows name the same one
- live: int32 [8], P('section'), may hold values from 1 to 16
Outputs:
- grad_up: bfloat16 [8, 5120, 10240], P('section', None, 'peer')
- returned: bfloat16 [8192, 5120], P(('section', 'peer'))
The draws below stay inside these ranges and needn't reach their ends.
Inputs may be any that keep to these rules, and one draw needn't show every extreme that they name: `senders`: in each section's 16 rows no peer is named more than 2 times, a bound that some block reaches.
All inputs are finite; a program needn't handle non-finite values.
Results may differ from the reference program's by a relative error of at most 0.0065.
Values may be sent and summed in bfloat16 or wider, within the bound.
A program may use at most 128 MiB of HBM per device.

```python
import math
import jax
import jax.numpy as jnp
import numpy as np
from jax import lax

D = 5120
FF = 10240
MB = 16
MB_TOK = 32
CAP = 2
ROWS = 512
TOKENS = 4096
SLOTS = 8192
N_SECTION = 8
N_PEER = 16


def draw_acts(key, part):
    key = jax.random.fold_in(key, 11)
    first, second = jax.random.split(key, 2)
    column = jnp.exp(jax.random.uniform(second, (1, D), jnp.float32, 0.0, math.log(10.0)))
    base = jnp.clip(jax.random.normal(first, (TOKENS, D), jnp.float32), -4.5, 4.5)
    return (base * column).astype(jnp.bfloat16)


def place_ends(values, stream_key, least, high):
    longest = values.shape.index(max(values.shape))
    spots = []
    for shift in (0, 1):
        where = [jax.random.randint(jax.random.fold_in(stream_key, axis), (), 0, length) for axis, length in enumerate(values.shape)]
        where[longest] = (where[longest] + shift) % values.shape[longest]
        spots.append(tuple(where))
    return values.at[spots[0]].set(least).at[spots[1]].set(high)


def shard_levels(key, shape, pieces, smallest, largest):
    level, own = 1.0, jax.random.fold_in(key, 6)
    for axis_at, parts in pieces:
        draws = jnp.exp(jax.random.uniform(jax.random.fold_in(own, axis_at), (parts,), jnp.float32, smallest / len(pieces), largest / len(pieces)))
        level = level * jnp.repeat(draws, shape[axis_at] // parts).reshape([-1 if axis == axis_at else 1 for axis in range(len(shape))])
    return level


def assign_block(own_key, own, number, rows, number_of, top, reach, skew):
    order = jax.random.permutation(own_key, number_of)
    crowded, ordinary = portions_of(number_of, rows * top, reach, skew, True), portions_of(number_of, rows * top, reach, skew, False)
    places = jnp.arange(number_of)

    def named(tallies, turn):
        used = int((tallies > 0).sum())
        fixed = max(1, used // 4)
        moved = fixed + (places - fixed + turn * (used - fixed)) % max(1, number_of - fixed)
        return jnp.zeros((number_of,), jnp.int32).at[order[jnp.where(places < fixed, places, moved)]].set(jnp.asarray(tallies, jnp.int32))

    tallies = jnp.where(number % 4 == 0, named(crowded, number // 4), named(ordinary, number - number // 4 - 1))
    mixed = jax.random.permutation(jax.random.fold_in(own, 3), number_of)
    source_of, taker = mixed[0:number_of // 2 * 2:2], mixed[1:number_of // 2 * 2:2]
    slack = jnp.minimum(tallies[source_of] - 1, reach - tallies[taker]) // 2
    slack = jnp.where((source_of == order[0]) | (taker == order[0]) | (tallies[taker] == 0), 0, jnp.maximum(slack, 0))
    moved = jax.random.randint(jax.random.fold_in(own, 4), (number_of // 2,), 0, 1 << 20) % (slack + 1)
    tallies = tallies.at[source_of].add(-moved).at[taker].add(moved)
    members = jnp.searchsorted(jnp.cumsum(tallies), jnp.arange(rows * top), side="right").astype(jnp.int32)
    table = members.reshape(top, rows).T
    table = table[jax.random.permutation(jax.random.fold_in(own, 1), rows)]
    turn = jax.random.randint(jax.random.fold_in(own, 2), (rows, 1), 0, top)
    return jnp.take_along_axis(table, (jnp.arange(top)[None, :] + turn) % top, axis=1)


def portions_of(count, total, limit, skew, full):
    weights = [(1 << 20) // math.isqrt(standing ** skew) + 1 for standing in range(1, count + 1)]
    largest = limit if full else min(limit, max(-(-total // count), total * weights[0] // sum(weights)))
    least = 1 if total - largest >= count - 1 else 0
    counts, spare = [largest] + [least] * (count - 1), total - largest - least * (count - 1)
    while spare > 0:
        candidates = [i for i in range(1, count) if counts[i] < largest] or [i for i in range(1, count) if counts[i] < limit]
        whole, left = sum([weights[i] for i in candidates]), spare
        for i in candidates:
            extra = min(limit - counts[i], max(1, left * weights[i] // whole), spare)
            counts[i] = counts[i] + extra
            spare = spare - extra
    return np.array(counts)


def scatter_about(rng, shape, width, limit, pieces=(), held_as=jnp.bfloat16):
    factor_of = shard_levels(rng, shape, pieces, -0.22, 0.18) if pieces else 1.0
    array = jax.random.normal(rng, shape, jnp.float32) * width * factor_of
    return jnp.minimum(jnp.maximum(array, -limit), limit).astype(held_as)


def setup_inputs(seed: int = 0) -> dict:
    keys = jax.random.split(jax.random.key(seed), 8)
    acts = draw_acts(jax.random.fold_in(keys[7], 71), 0)
    grad_out = scatter_about(keys[1], (TOKENS, D), 1.0, 6.0, ((0, 8), (1, 16)))
    gain = jnp.clip(1.0 + 0.18 * jax.random.normal(keys[2], (N_SECTION, D), jnp.float32), 0.099609375, 1.8984375).astype(jnp.bfloat16)
    w_up = scatter_about(keys[3], (N_SECTION, D, FF), D ** -0.5, 0.078125, ((0, 8), (2, 16)))
    w_down = scatter_about(keys[4], (N_SECTION, FF, D), FF ** -0.5, 0.0625, ((0, 8), (1, 16)))
    senders_keys = jax.random.split(jax.random.fold_in(keys[5], 1), (N_SECTION * MB) // MB)
    senders_turns = jax.random.permutation(jax.random.fold_in(keys[5], 3), (N_SECTION * MB) // MB)
    senders = jax.vmap(lambda own, number: assign_block(jax.random.fold_in(keys[5], 2), own, number, MB, N_PEER, 1, CAP, 1))(senders_keys, senders_turns).reshape((N_SECTION * MB, 1))
    live = place_ends(jax.random.randint(keys[6], (N_SECTION,), 1, MB + 1), jax.random.fold_in(keys[6], 1), 1, MB).astype(jnp.int32)
    return dict(acts=acts, grad_out=grad_out, gain=gain, w_up=w_up, w_down=w_down, senders=senders, live=live)


def norm_back(summed, normed, gain_f, rstd, grad_rows):
    scaled_grad = summed * gain_f
    first = lax.optimization_barrier(jnp.mean(scaled_grad, axis=-1, keepdims=True))
    second = lax.optimization_barrier(jnp.mean(scaled_grad * normed, axis=-1, keepdims=True))
    total = rstd * (scaled_grad - first - normed * second) + grad_rows.astype(jnp.float32)
    return total.astype(jnp.bfloat16)

def slot_index(section_list):
    same = section_list[:, None] == section_list[None, :]
    earlier = jnp.arange(MB)[None, :] < jnp.arange(MB)[:, None]
    rank = lax.optimization_barrier(jnp.sum((same & earlier).astype(jnp.int32), axis=1)).astype(jnp.int32)
    return (section_list * CAP + rank).astype(jnp.int32)

def section_pass(inputs):
    acts, grad_out, gain, w_up, w_down, live = inputs
    rows = acts.shape[0]
    alive = (jnp.arange(rows) // MB_TOK < live).astype(jnp.float32)[:, None]
    values = acts.astype(jnp.float32)
    mean = lax.optimization_barrier(jnp.mean(values, axis=-1, keepdims=True))
    centre = values - mean
    rstd = lax.rsqrt(lax.optimization_barrier(jnp.mean(centre * centre, axis=-1, keepdims=True)) + 1e-05)
    normed = centre * rstd
    gain_f = gain.astype(jnp.float32)[None, :]
    scaled = (normed * gain_f).astype(jnp.bfloat16)
    grad_live = (grad_out.astype(jnp.float32) * alive).astype(jnp.bfloat16)
    pre = jnp.dot(scaled, w_up, preferred_element_type=jnp.float32)
    slope = 0.5 * (1.0 + lax.erf(pre * 0.7071067811865476)) + pre * jnp.exp(-0.5 * pre * pre) * 0.3989422804014327
    back_hidden = jnp.dot(grad_live, w_down.T, preferred_element_type=jnp.float32)
    back_pre = (back_hidden * slope).astype(jnp.bfloat16)
    count = live.astype(jnp.float32)
    grad_up = (jnp.dot(scaled.T, back_pre, preferred_element_type=jnp.float32) / count).astype(jnp.bfloat16)
    group = FF // N_PEER
    parts_pre = back_pre.reshape(rows, N_PEER, group)
    parts_w = w_up.reshape(D, N_PEER, group)

    def add_part(total, index):
        term = jnp.dot(parts_pre[:, index], parts_w[:, index].T, preferred_element_type=jnp.float32)
        term = lax.optimization_barrier(term.astype(jnp.bfloat16)).astype(jnp.float32)
        return (total + term, None)
    summed, _ = lax.scan(add_part, jnp.zeros((rows, D), jnp.float32), jnp.arange(N_PEER))
    input_grad = norm_back(summed, normed, gain_f, rstd, grad_live)
    return (grad_up, input_grad)

def reference(acts, grad_out, gain, w_up, w_down, senders, live):
    acts_st = acts.reshape(N_SECTION, ROWS, D)
    grad_st = grad_out.reshape(N_SECTION, ROWS, D)
    grad_up, input_grad = lax.map(section_pass, (acts_st, grad_st, gain, w_up, w_down, live))
    lists = senders[:, 0].reshape(N_SECTION, MB)

    def route(pair):
        section_list, grads = pair
        target = slot_index(section_list)
        blank = jnp.zeros((N_PEER * CAP, MB_TOK, D), jnp.bfloat16)
        return blank.at[target].set(grads.reshape(MB, MB_TOK, D))
    routed = lax.map(route, (lists, input_grad))
    shifted = jnp.concatenate([routed[1:], jnp.zeros((1, N_PEER * CAP, MB_TOK, D), jnp.bfloat16)], axis=0)
    returned = shifted.reshape(SLOTS, D)
    return (grad_up, returned)
```

```python
import functools

import jax
import jax.numpy as jnp
from jax import lax
from jax.experimental import pallas as pl
from jax.experimental.pallas import tpu as pltpu
from jax.sharding import PartitionSpec as P

MESH = pl.DeviceIdType.MESH
F32 = jnp.float32
BF16 = jnp.bfloat16
MB = 16
MB_TOK = 32
ROWS = 512
HALF = 256
QUART = 128
D = 5120
CHIP = 640
LOCAL = 320
CHIPS = 8
MIB = 2**20

MATES = [(0, 1), (0, 2), (0, 3), (1, 0), (1, 1), (1, 2), (1, 3)]
GATHER_ORDER = [(0, 0), (1, 0), (0, 3), (0, 1), (0, 2), (1, 3), (1, 1), (1, 2)]
SUM_ORDER = [(1, 2), (1, 1), (1, 3), (0, 1), (0, 3), (0, 2), (1, 0), (0, 0)]
LAG = 3

N_AG = 19


def nt_dot(a, b):
    return lax.dot_general(a, b, (((1,), (1,)), ((), ())), preferred_element_type=F32)


def pick(table, k):
    out = table[0]
    for i in range(1, len(table)):
        out = jnp.where(k == i, table[i], out)
    return out


def place():
    s = lax.axis_index("section")
    p = lax.axis_index("peer")
    q = p // 2
    return s, q // 4, q % 4, p % 2


def layer_kernel(
    acts_ref, grad_ref, gain_ref, live_ref, wu_hbm, wd_hbm,
    compact_ref, x_hbm, bp_hbm,
    wu, wd, g_all, x_all, pre, bh, bp, part, sib_part, r_a, r_b, r_c, r_e, r_d,
    gl, sib_gl, sib_acts, my_gain, sib_gain, normed, facts, sums, sib_sums,
    all_sums, out_buf,
    ag_send, ag_recv, own_send, own_recv, facts_send, facts_recv, sums_send, sums_recv,
    sib_send, sib_recv, rs_send, rs_recv, local_sem,
):
    s, z, y, c = place()
    z2, yp, ym, y2 = 1 - z, (y + 1) % 4, (y + 3) % 4, (y + 2) % 4
    oc = 1 - c
    q_me = z * 4 + y

    def dev(zz, yy, cc):
        return (s, (zz * 4 + yy) * 2 + cc)

    def rows(lane, half=None):
        if half is None:
            return pl.ds(pl.multiple_of(lane * HALF, HALF), HALF)
        return pl.ds(pl.multiple_of(lane * HALF + half * QUART, QUART), QUART)

    sends = []

    def remote(src, dst, ssem, rsem, where):
        return pltpu.make_async_remote_copy(
            src_ref=src, dst_ref=dst, send_sem=ssem, recv_sem=rsem,
            device_id=where, device_id_type=MESH,
        )

    def send(src, dst, ssem, rsem, where):
        copy = remote(src, dst, ssem, rsem, where)
        copy.start()
        sends.append(copy)

    def recv(dst, ssem, rsem):
        remote(dst, dst, ssem, rsem, dev(z, y, oc)).wait_recv()

    load_wd = pltpu.make_async_copy(wd_hbm.at[0], wd, local_sem.at[0])
    load_wu = pltpu.make_async_copy(wu_hbm.at[0], wu, local_sem.at[1])
    load_wd.start()
    load_wu.start()

    barrier = pltpu.get_barrier_semaphore()
    pl.semaphore_signal(barrier, inc=1, device_id=dev(z, y, oc), device_id_type=MESH)
    for dz, dy in MATES:
        pl.semaphore_signal(
            barrier, inc=1, device_id=dev((z + dz) % 2, (y + dy) % 4, c), device_id_type=MESH
        )
    pl.semaphore_wait(barrier, 8)

    token = lax.broadcasted_iota(jnp.int32, (ROWS, LOCAL), 0) // MB_TOK
    alive = (token < live_ref[0]).astype(F32)
    gl[...] = (grad_ref[...].astype(F32) * alive).astype(BF16)
    send(gl.at[rows(oc)], sib_gl, own_send.at[0], own_recv.at[0], dev(z, y, oc))
    send(acts_ref.at[rows(oc)], sib_acts, own_send.at[1], own_recv.at[1], dev(z, y, oc))
    my_gain[...] = jnp.broadcast_to(gain_ref[...].astype(F32), (8, LOCAL))
    send(my_gain, sib_gain, own_send.at[2], own_recv.at[2], dev(z, y, oc))

    def side_by_side(mine, other):
        left = jnp.where(c == 0, mine, other)
        right = jnp.where(c == 0, other, mine)
        return jnp.concatenate([left, right], axis=1)

    bufs = (g_all, x_all)

    def block(a, zz, yy, lane, half=None):
        return bufs[a].at[zz * 4 + yy, rows(lane, half)]

    def ag_start(a, tag, zz, yy, where, half=None):
        ref = block(a, zz, yy, c, half)
        send(ref, ref, ag_send.at[a, tag], ag_recv.at[a, tag], where)

    def ag_wait(a, tag, zz, yy, lane, half=None):
        recv(block(a, zz, yy, lane, half), ag_send.at[a, tag], ag_recv.at[a, tag])

    def ag_own(a):
        ag_start(a, 0, z, y, dev(z2, y, c))
        ag_start(a, 1, z, y, dev(z, yp, c))
        ag_start(a, 2, z, y, dev(z, ym, c))
        ag_start(a, 9, z, y, dev(z, y, oc))

    def ag_second(a):
        ag_wait(a, 1, z, ym, c)
        ag_start(a, 3, z, ym, dev(z, yp, c), 0)
        ag_wait(a, 2, z, yp, c)
        ag_start(a, 4, z, yp, dev(z, ym, c), 1)
        ag_wait(a, 0, z2, y, c)
        ag_start(a, 5, z2, y, dev(z, yp, c))
        ag_start(a, 6, z2, y, dev(z, ym, c))
        ag_start(a, 10, z, ym, dev(z, y, oc))
        ag_start(a, 11, z, yp, dev(z, y, oc))
        ag_start(a, 12, z2, y, dev(z, y, oc))

    def ag_second_sib(a):
        ag_wait(a, 10, z, ym, oc)
        ag_wait(a, 11, z, yp, oc)
        ag_wait(a, 12, z2, y, oc)

    def ag_third(a):
        ag_wait(a, 3, z, y2, c, 0)
        ag_start(a, 7, z, y2, dev(z2, y, c), 0)
        ag_wait(a, 4, z, y2, c, 1)
        ag_start(a, 8, z, y2, dev(z2, y, c), 1)
        ag_start(a, 13, z, y2, dev(z, y, oc), 0)
        ag_start(a, 14, z, y2, dev(z, y, oc), 1)

    def ag_fourth(a):
        ag_wait(a, 5, z2, ym, c)
        ag_start(a, 15, z2, ym, dev(z, y, oc))
        ag_wait(a, 6, z2, yp, c)
        ag_start(a, 16, z2, yp, dev(z, y, oc))
        ag_wait(a, 7, z2, y2, c, 0)
        ag_start(a, 17, z2, y2, dev(z, y, oc), 0)
        ag_wait(a, 8, z2, y2, c, 1)
        ag_start(a, 18, z2, y2, dev(z, y, oc), 1)

    def ag_fourth_sib(a):
        ag_wait(a, 13, z, y2, oc, 0)
        ag_wait(a, 14, z, y2, oc, 1)
        ag_wait(a, 17, z2, y2, oc, 0)
        ag_wait(a, 18, z2, y2, oc, 1)
        ag_wait(a, 15, z2, ym, oc)
        ag_wait(a, 16, z2, yp, oc)

    def chip_at(table, k):
        dz = pick([t[0] for t in table], k)
        dy = pick([t[1] for t in table], k)
        return ((z + dz) % 2) * 4 + (y + dy) % 4

    def columns(q):
        return pl.ds(pl.multiple_of(q * CHIP, CHIP), CHIP)

    def mul_g(lo, hi):
        @pl.loop(lo, hi)
        def _(k):
            q = chip_at(GATHER_ORDER, k)
            term = nt_dot(g_all[q], wd[:, columns(q)])
            if lo == 0:
                bh[...] = term
            else:
                bh[...] += term

    def mul_x(lo, hi):
        @pl.loop(lo, hi)
        def _(k):
            q = chip_at(GATHER_ORDER, k)
            term = jnp.dot(x_all[q], wu[columns(q), :], preferred_element_type=F32)
            if lo == 0:
                pre[...] = term
            else:
                pre[...] += term

    recv(sib_gl, own_send.at[0], own_recv.at[0])
    g_all[q_me, rows(c)] = side_by_side(
        gl[rows(c)].astype(F32), sib_gl[...].astype(F32)
    ).astype(BF16)
    ag_own(0)

    recv(sib_acts, own_send.at[1], own_recv.at[1])
    recv(sib_gain, own_send.at[2], own_recv.at[2])
    values = side_by_side(acts_ref[rows(c)].astype(F32), sib_acts[...].astype(F32))
    gain_chip = side_by_side(my_gain[...], sib_gain[...])
    mean_here = jnp.mean(values, axis=1, keepdims=True)
    spread = values - mean_here
    square_here = jnp.sum(spread * spread, axis=1, keepdims=True)
    lane_at = lax.broadcasted_iota(jnp.int32, (HALF, 128), 1)
    table = jnp.where(lane_at == 0, mean_here, jnp.where(lane_at == 1, square_here, 0.0))
    facts[q_me, :, 0:HALF] = table.T[0:8]
    facts[q_me, :, HALF:] = gain_chip
    for i, (dz, dy) in enumerate(MATES):
        send(
            facts.at[q_me], facts.at[q_me], facts_send.at[i], facts_recv.at[i],
            dev((z + dz) % 2, (y + dy) % 4, c),
        )
    normed[...] = values

    def columns_of(first_row, second_row):
        tall = jnp.concatenate(
            [first_row, second_row, jnp.zeros((126, HALF), F32)], axis=0
        ).T
        return tall[:, 0:1], tall[:, 1:2]

    for i, (dz, dy) in enumerate(MATES):
        recv(facts.at[((z + dz) % 2) * 4 + (y + 4 - dy) % 4], facts_send.at[i], facts_recv.at[i])
    means = [facts[i, 0:1, 0:HALF] for i in range(CHIPS)]
    mean_row = sum(means) / CHIPS
    square_row = sum(facts[i, 1:2, 0:HALF] for i in range(CHIPS))
    square_row += CHIP * sum((m - mean_row) * (m - mean_row) for m in means)
    rstd_row = lax.rsqrt(square_row / D + 1e-05)
    mean_col, rstd_col = columns_of(mean_row, rstd_row)
    normed[...] = (normed[...] - mean_col) * rstd_col
    x_all[q_me, rows(c)] = (normed[...] * facts[q_me, 0:1, HALF:]).astype(BF16)
    ag_own(1)

    load_wd.wait()
    ag_wait(0, 9, z, y, oc)
    mul_g(0, 1)
    ag_second(0)
    load_wu.wait()
    ag_wait(1, 9, z, y, oc)
    mul_x(0, 1)
    ag_second_sib(0)
    mul_g(1, 4)
    ag_second(1)
    ag_third(0)
    ag_second_sib(1)
    mul_x(1, 4)
    weight_sum = jnp.zeros((16, CHIP), F32)
    for i in range(CHIPS):
        gain_i = jnp.broadcast_to(facts[i, 0:1, HALF:], (16, CHIP)).astype(BF16)
        weight_sum += jnp.dot(gain_i, wu[i * CHIP : (i + 1) * CHIP], preferred_element_type=F32)
    ag_third(1)
    ag_fourth(0)
    ag_fourth_sib(0)
    mul_g(4, 8)
    ag_fourth(1)
    ag_fourth_sib(1)
    mul_x(4, 8)
    save_x = pltpu.make_async_copy(x_all, x_hbm, local_sem.at[2])
    save_x.start()

    weight_row = weight_sum[0:1]

    @pl.loop(0, ROWS // 128)
    def _(i):
        at = pl.ds(pl.multiple_of(i * 128, 128), 128)
        p = pre[at]
        slope = (
            0.5 * (1.0 + lax.erf(p * 0.7071067811865476))
            + p * jnp.exp(-0.5 * p * p) * 0.3989422804014327
        )
        b = (bh[at] * slope).astype(BF16)
        bp[at] = b
        b = b.astype(F32)
        first = jnp.sum(b * weight_row, axis=1, keepdims=True)
        second = jnp.sum(b * p, axis=1, keepdims=True)
        lane = lax.broadcasted_iota(jnp.int32, (128, 128), 1)
        both = jnp.where(lane == 0, first, jnp.where(lane == 1, second, 0.0))
        sums[i // 2, i % 2] = both.T[0:8]

    save_bp = pltpu.make_async_copy(bp, bp_hbm, local_sem.at[3])
    save_bp.start()
    send(sums.at[oc], sib_sums, sums_send.at[7], sums_recv.at[7], dev(z, y, oc))

    def sib_copy(q):
        return remote(
            part.at[q, rows(oc)], sib_part.at[q], sib_send.at[q], sib_recv.at[q], dev(z, y, oc)
        )

    def rs_start(tag, src, dst, where):
        send(src, dst, rs_send.at[tag], rs_recv.at[tag], where)

    def rs_wait(tag, dst):
        recv(dst, rs_send.at[tag], rs_recv.at[tag])

    def chip(zz, yy):
        return zz * 4 + yy

    q_p, q_m, q_2 = chip(z, yp), chip(z, ym), chip(z, y2)
    q_z, q_zp, q_zm, q_z2 = chip(z2, y), chip(z2, yp), chip(z2, ym), chip(z2, y2)
    h0, h1 = pl.ds(0, QUART), pl.ds(QUART, QUART)

    def multiply(k):
        q = chip_at(SUM_ORDER, k)
        part[q] = nt_dot(bp[...], wu[columns(q), :]).astype(BF16)
        sib_copy(q).start()

    def join(k):
        q = chip_at(SUM_ORDER, k)
        sib_copy(q).wait_recv()
        part[q, rows(c)] = (part[q, rows(c)].astype(F32) + sib_part[q].astype(F32)).astype(BF16)

    @pl.loop(0, LAG)
    def _(k):
        multiply(k)

    @pl.loop(LAG, CHIPS)
    def _(k):
        multiply(k)
        join(k - LAG)

        @pl.when(k == LAG)
        def _():
            remote(part.at[q_z2, rows(c)], r_a, rs_send.at[0], rs_recv.at[0], dev(z2, y, c)).start()

        @pl.when(k == LAG + 1)
        def _():
            remote(
                part.at[q_zp, rows(c)], r_b.at[0], rs_send.at[1], rs_recv.at[1], dev(z, yp, c)
            ).start()

        @pl.when(k == LAG + 2)
        def _():
            remote(
                part.at[q_zm, rows(c)], r_b.at[1], rs_send.at[2], rs_recv.at[2], dev(z, ym, c)
            ).start()

        @pl.when(k == LAG + 3)
        def _():
            remote(
                part.at[q_p, rows(c, 1)], r_e.at[0, h1], rs_send.at[3], rs_recv.at[3],
                dev(z, yp, c),
            ).start()

        @pl.when(k == LAG + 4)
        def _():
            remote(
                part.at[q_m, rows(c, 0)], r_e.at[1, h0], rs_send.at[4], rs_recv.at[4],
                dev(z, ym, c),
            ).start()

    @pl.loop(CHIPS - LAG, CHIPS)
    def _(k):
        join(k)

    sends.extend(
        [
            remote(part.at[q_z2, rows(c)], r_a, rs_send.at[0], rs_recv.at[0], dev(z2, y, c)),
            remote(part.at[q_zp, rows(c)], r_b.at[0], rs_send.at[1], rs_recv.at[1], dev(z, yp, c)),
            remote(part.at[q_zm, rows(c)], r_b.at[1], rs_send.at[2], rs_recv.at[2], dev(z, ym, c)),
            remote(part.at[q_p, rows(c, 1)], r_e.at[0, h1], rs_send.at[3], rs_recv.at[3], dev(z, yp, c)),
            remote(part.at[q_m, rows(c, 0)], r_e.at[1, h0], rs_send.at[4], rs_recv.at[4], dev(z, ym, c)),
        ]
    )

    recv(sib_sums, sums_send.at[7], sums_recv.at[7])
    all_sums[q_me] = sums[c] + sib_sums[...]
    for i, (dz, dy) in enumerate(MATES):
        send(
            all_sums.at[q_me], all_sums.at[q_me], sums_send.at[i], sums_recv.at[i],
            dev((z + dz) % 2, (y + dy) % 4, c),
        )

    rs_wait(0, r_a)
    part[q_2, rows(c)] = (part[q_2, rows(c)].astype(F32) + r_a[...].astype(F32)).astype(BF16)
    rs_start(5, part.at[q_2, rows(c, 0)], r_c.at[0], dev(z, yp, c))
    rs_start(6, part.at[q_2, rows(c, 1)], r_c.at[1], dev(z, ym, c))
    rs_wait(1, r_b.at[0])
    rs_wait(2, r_b.at[1])
    part[q_z, rows(c)] = (
        part[q_z, rows(c)].astype(F32) + r_b[0].astype(F32) + r_b[1].astype(F32)
    ).astype(BF16)
    rs_start(7, part.at[q_z, rows(c)], r_d, dev(z2, y, c))
    rs_wait(5, r_c.at[0])
    part[q_p, rows(c, 0)] = (part[q_p, rows(c, 0)].astype(F32) + r_c[0].astype(F32)).astype(BF16)
    rs_start(8, part.at[q_p, rows(c, 0)], r_e.at[0, h0], dev(z, yp, c))
    rs_wait(6, r_c.at[1])
    part[q_m, rows(c, 1)] = (part[q_m, rows(c, 1)].astype(F32) + r_c[1].astype(F32)).astype(BF16)
    rs_start(9, part.at[q_m, rows(c, 1)], r_e.at[1, h1], dev(z, ym, c))

    for i, (dz, dy) in enumerate(MATES):
        recv(
            all_sums.at[((z + dz) % 2) * 4 + (y + 4 - dy) % 4], sums_send.at[i], sums_recv.at[i]
        )
    total_sums = sum(all_sums[i] for i in range(CHIPS)) / D
    row_first = jnp.concatenate([total_sums[0, 0:1], total_sums[1, 0:1]], axis=1)
    row_second = jnp.concatenate([total_sums[0, 1:2], total_sums[1, 1:2]], axis=1)
    first_col, second_col = columns_of(row_first, row_second)

    rs_wait(7, r_d)
    rs_wait(3, r_e.at[0, h1])
    rs_wait(4, r_e.at[1, h0])
    rs_wait(8, r_e.at[0, h0])
    rs_wait(9, r_e.at[1, h1])
    summed = (
        part[q_me, rows(c)].astype(F32)
        + r_d[...].astype(F32)
        + r_e[0].astype(F32)
        + r_e[1].astype(F32)
    )
    scaled_grad = summed * facts[q_me, 0:1, HALF:]
    total = rstd_col * (scaled_grad - first_col - normed[...] * second_col)
    out_buf[...] = (total + g_all[q_me, rows(c)].astype(F32)).astype(BF16)
    save_out = pltpu.make_async_copy(out_buf, compact_ref, local_sem.at[4])
    save_out.start()

    @pl.loop(0, CHIPS)
    def _(k):
        sib_copy(k).wait_send()

    for copy in sends:
        copy.wait_send()
    save_x.wait()
    save_bp.wait()
    save_out.wait()


def layer(acts, grad_out, gain, live, w_up, w_down):
    vmem, anyspace = pl.BlockSpec(memory_space=pltpu.VMEM), pl.BlockSpec(memory_space=pl.ANY)
    dma = pltpu.SemaphoreType.DMA
    return pl.pallas_call(
        layer_kernel,
        out_shape=[
            jax.ShapeDtypeStruct((HALF, CHIP), BF16),
            jax.ShapeDtypeStruct((CHIPS, ROWS, CHIP), BF16),
            jax.ShapeDtypeStruct((ROWS, CHIP), BF16),
        ],
        in_specs=[vmem, vmem, vmem, pl.BlockSpec(memory_space=pltpu.SMEM), anyspace, anyspace],
        out_specs=[anyspace, anyspace, anyspace],
        scratch_shapes=[
            pltpu.VMEM((D, CHIP), BF16),
            pltpu.VMEM((CHIP, D), BF16),
            pltpu.VMEM((CHIPS, ROWS, CHIP), BF16),
            pltpu.VMEM((CHIPS, ROWS, CHIP), BF16),
            pltpu.VMEM((ROWS, CHIP), F32),
            pltpu.VMEM((ROWS, CHIP), F32),
            pltpu.VMEM((ROWS, CHIP), BF16),
            pltpu.VMEM((CHIPS, ROWS, CHIP), BF16),
            pltpu.VMEM((CHIPS, HALF, CHIP), BF16),
            pltpu.VMEM((HALF, CHIP), BF16),
            pltpu.VMEM((2, HALF, CHIP), BF16),
            pltpu.VMEM((2, QUART, CHIP), BF16),
            pltpu.VMEM((2, HALF, CHIP), BF16),
            pltpu.VMEM((HALF, CHIP), BF16),
            pltpu.VMEM((ROWS, LOCAL), BF16),
            pltpu.VMEM((HALF, LOCAL), BF16),
            pltpu.VMEM((HALF, LOCAL), BF16),
            pltpu.VMEM((8, LOCAL), F32),
            pltpu.VMEM((8, LOCAL), F32),
            pltpu.VMEM((HALF, CHIP), F32),
            pltpu.VMEM((CHIPS, 8, HALF + CHIP), F32),
            pltpu.VMEM((2, 2, 8, 128), F32),
            pltpu.VMEM((2, 8, 128), F32),
            pltpu.VMEM((CHIPS, 2, 8, 128), F32),
            pltpu.VMEM((HALF, CHIP), BF16),
            dma((2, N_AG)),
            dma((2, N_AG)),
            dma((3,)),
            dma((3,)),
            dma((7,)),
            dma((7,)),
            dma((8,)),
            dma((8,)),
            dma((CHIPS,)),
            dma((CHIPS,)),
            dma((10,)),
            dma((10,)),
            dma((5,)),
        ],
        compiler_params=pltpu.CompilerParams(
            collective_id=0, has_side_effects=True, vmem_limit_bytes=56 * MIB
        ),
        cost_estimate=pl.CostEstimate(
            flops=6 * ROWS * D * CHIP, bytes_accessed=20 * MIB, transcendentals=2 * ROWS * CHIP
        ),
    )(acts, grad_out, gain, live, w_up, w_down)


def route_kernel(
    compact_ref, senders_ref, out_ref,
    full, stage, landed,
    sib_send, sib_recv, put_send, put_recv,
):
    s, z, y, c = place()
    oc = 1 - c
    q_me = z * 4 + y

    def dev(zz, yy, cc):
        return (s, (zz * 4 + yy) * 2 + cc)

    def remote(src, dst, ssem, rsem, where):
        return pltpu.make_async_remote_copy(
            src_ref=src, dst_ref=dst, send_sem=ssem, recv_sem=rsem,
            device_id=where, device_id_type=MESH,
        )

    barrier = pltpu.get_barrier_semaphore()
    pl.semaphore_signal(barrier, inc=1, device_id=dev(z, y, oc), device_id_type=MESH)
    for dz, dy in MATES:
        pl.semaphore_signal(
            barrier, inc=1, device_id=dev((z + dz) % 2, (y + dy) % 4, c), device_id_type=MESH
        )
    pl.semaphore_wait(barrier, 8)

    mine = pl.ds(pl.multiple_of(c * HALF, HALF), HALF)
    other = pl.ds(pl.multiple_of(oc * HALF, HALF), HALF)
    sib = remote(compact_ref, full.at[mine], sib_send, sib_recv, dev(z, y, oc))
    sib.start()
    full[mine] = compact_ref[...]

    base = jnp.minimum(s + 1, lax.axis_size("section") - 1) * MB
    names = [senders_ref[base + m] for m in range(MB)]

    token = lax.broadcasted_iota(jnp.int32, (2 * MB_TOK, ROWS), 1)
    slot_row = token % MB_TOK
    for m in range(MB):
        rank = jnp.int32(0)
        for before in range(m):
            rank = rank + jnp.where(names[before] == names[m], 1, 0)
        slot_row += jnp.where(token // MB_TOK == m, (names[m] * 2 + rank) * MB_TOK, 0)
    row = lax.broadcasted_iota(jnp.int32, (2 * MB_TOK, ROWS), 0)

    remote(full.at[other], full.at[other], sib_send, sib_recv, dev(z, y, oc)).wait_recv()

    def fill(dz, dy):
        peer = (((z + dz) % 2) * 4 + (y + dy) % 4) * 2 + c
        chosen = jnp.where(slot_row == row + peer * (2 * MB_TOK), 1.0, 0.0).astype(BF16)
        return jnp.dot(chosen, full[...], preferred_element_type=F32).astype(BF16)

    puts = []
    columns = pl.ds(pl.multiple_of(q_me * CHIP, CHIP), CHIP)
    for i, (dz, dy) in enumerate(MATES):
        stage[i] = fill(dz, dy)
        put = remote(
            stage.at[i], landed.at[:, columns], put_send.at[i], put_recv.at[i],
            dev((z + dz) % 2, (y + dy) % 4, c),
        )
        put.start()
        puts.append(put)
    landed[:, columns] = fill(0, 0)
    for i, (dz, dy) in enumerate(MATES):
        q = ((z + dz) % 2) * 4 + (y + 4 - dy) % 4
        there = landed.at[:, pl.ds(pl.multiple_of(q * CHIP, CHIP), CHIP)]
        remote(there, there, put_send.at[i], put_recv.at[i], dev(z, y, oc)).wait_recv()
    out_ref[...] = landed[...]
    sib.wait_send()
    for put in puts:
        put.wait_send()


def route(compact, senders):
    vmem = pl.BlockSpec(memory_space=pltpu.VMEM)
    dma = pltpu.SemaphoreType.DMA
    return pl.pallas_call(
        route_kernel,
        out_shape=jax.ShapeDtypeStruct((2 * MB_TOK, D), BF16),
        in_specs=[vmem, pl.BlockSpec(memory_space=pltpu.SMEM)],
        out_specs=vmem,
        scratch_shapes=[
            pltpu.VMEM((ROWS, CHIP), BF16),
            pltpu.VMEM((7, 2 * MB_TOK, CHIP), BF16),
            pltpu.VMEM((2 * MB_TOK, D), BF16),
            dma,
            dma,
            dma((7,)),
            dma((7,)),
        ],
        compiler_params=pltpu.CompilerParams(
            collective_id=1, has_side_effects=True, vmem_limit_bytes=16 * MIB
        ),
    )(compact, senders)


def body(acts, grad_out, gain, w_up, w_down, senders, live):
    compact, scaled, back_pre = layer(acts, grad_out, gain, live, w_up, w_down)
    length = lax.axis_size("section")
    shifted = lax.ppermute(compact, "section", [(i, i - 1) for i in range(1, length)])
    grad_up = lax.dot_general(
        scaled, back_pre, (((1,), (0,)), ((), ())), preferred_element_type=F32
    ).reshape(D, CHIP)
    grad_up = (grad_up / live[0].astype(F32)).astype(BF16)[None]
    returned = route(shifted, senders[:, 0])
    return (grad_up, returned)


def solution(mesh):
    in_specs = (
        P("section", "peer"),
        P("section", "peer"),
        P("section", "peer"),
        P("section", None, "peer"),
        P("section", "peer", None),
        P(),
        P("section"),
    )
    out_specs = (P("section", None, "peer"), P(("section", "peer"), None))
    return jax.shard_map(body, mesh=mesh, in_specs=in_specs, out_specs=out_specs, check_vma=False)
```

```python
import jax
import jax.numpy as jnp
from jax import lax
from jax.experimental import pallas as pl
from jax.experimental.pallas import tpu as pltpu
from jax.sharding import PartitionSpec as P

MESH = pl.DeviceIdType.MESH
F32 = jnp.float32
BF16 = jnp.bfloat16
MB = 16
MB_TOK = 32
ROWS = 512
TOKS = (256, 256)
FROM = (0, 256)
D = 5120
CHIP = 640
LOCAL = 320
PART = 160
CHIPS = 8
SLOT = 2 * MB_TOK
PIECE = 48
HEAD, TAIL = (0, PART), (PART, PART)
FIRST, BUT_FIRST = (0, PIECE), (PIECE, LOCAL - PIECE)
LAST, BUT_LAST = (LOCAL - PIECE, PIECE), (0, LOCAL - PIECE)
GU = 1280
MIB = 2**20

MATES = [(0, 1), (0, 2), (0, 3), (1, 0), (1, 1), (1, 2), (1, 3)]
SUM_ORDER = [(1, 2), (1, 1), (1, 3), (0, 1), (0, 3), (0, 2), (1, 0), (0, 0)]
LAG = 3
N_AG = 21
N_RS = 12


def nn_dot(a, b):
    return jnp.dot(a, b, preferred_element_type=F32)


def nt_dot(a, b):
    return lax.dot_general(a, b, (((1,), (1,)), ((), ())), preferred_element_type=F32)


def tn_dot(a, b):
    return lax.dot_general(a, b, (((0,), (0,)), ((), ())), preferred_element_type=F32)


def span(h):
    return slice(FROM[h], FROM[h] + TOKS[h])


def pick(table, k):
    out = table[0]
    for i in range(1, len(table)):
        out = jnp.where(k == i, table[i], out)
    return out


def layer_kernel(
    acts_hbm, grad_hbm, gain_ref, live_ref, senders_ref, wu_hbm, wd_hbm,
    gu_ref, returned_ref,
    wu, wd, g_all, x_all, pre, bh, bp, part, sib_part, r_a, r_b, r_c, r_e, r_d, r_p,
    acts, grads, normed, facts, my_facts, sib_facts, sums, sib_sums, all_sums, weight_rows,
    out_buf, moved, chosen, routed, stage, landed,
    ag_send, ag_recv, facts_send, facts_recv, sums_send, sums_recv,
    sib_send, sib_recv, rs_send, rs_recv, move_send, move_recv, put_send, put_recv,
    local_sem,
):
    s, p = lax.axis_index("section"), lax.axis_index("peer")
    q_me, c = p // 2, p % 2
    z, y, oc = q_me // 4, q_me % 4, 1 - c
    z2, yp, ym, y2 = 1 - z, (y + 1) % 4, (y + 3) % 4, (y + 2) % 4
    sections = lax.axis_size("section")

    def dev(zz, yy, cc):
        return (s, (zz * 4 + yy) * 2 + cc)

    def mate(i):
        dz, dy = MATES[i]
        return dev((z + dz) % 2, (y + dy) % 4, c)

    def mate_from(i):
        dz, dy = MATES[i]
        return ((z + dz) % 2) * 4 + (y + 4 - dy) % 4

    sibling = dev(z, y, oc)
    sends = []

    def remote(src, dst, ssem, rsem, where):
        return pltpu.make_async_remote_copy(
            src_ref=src, dst_ref=dst, send_sem=ssem, recv_sem=rsem,
            device_id=where, device_id_type=MESH,
        )

    def send(src, dst, ssem, rsem, where):
        copy = remote(src, dst, ssem, rsem, where)
        copy.start()
        sends.append(copy)

    def recv(dst, ssem, rsem):
        remote(dst, dst, ssem, rsem, sibling).wait_recv()

    def rows(at, count):
        return pl.ds(pl.multiple_of(at, 16), count)

    load_grad = pltpu.make_async_copy(grad_hbm, grads, local_sem.at[0])
    load_acts = pltpu.make_async_copy(acts_hbm, acts, local_sem.at[1])
    load_wd = pltpu.make_async_copy(wd_hbm.at[0], wd, local_sem.at[2])
    load_wu = pltpu.make_async_copy(wu_hbm.at[0], wu, local_sem.at[3])
    load_grad.start()
    load_acts.start()
    load_wd.start()
    load_wu.start()

    barrier = pltpu.get_barrier_semaphore()
    pl.semaphore_signal(barrier, inc=1, device_id=sibling, device_id_type=MESH)
    for i in range(7):
        pl.semaphore_signal(barrier, inc=1, device_id=mate(i), device_id_type=MESH)
    for step in (1, sections - 1):
        pl.semaphore_signal(
            barrier, inc=1, device_id=((s + step) % sections, p), device_id_type=MESH
        )
    pl.semaphore_wait(barrier, 10)

    bufs = (g_all, x_all)

    def block(a, h, zz, yy, cc, half=None):
        at = (zz * 4 + yy) * CHIP + cc * LOCAL
        first, count = (0, LOCAL) if half is None else half
        return bufs[a][h].at[rows(at + first, count)]

    def ag_start(a, h, tag, zz, yy, where, half=None):
        ref = block(a, h, zz, yy, c, half)
        send(ref, ref, ag_send.at[2 * a + h, tag], ag_recv.at[2 * a + h, tag], where)

    def ag_wait(a, h, tag, zz, yy, cc, half=None):
        recv(block(a, h, zz, yy, cc, half), ag_send.at[2 * a + h, tag], ag_recv.at[2 * a + h, tag])

    def ag_own(a, h):
        ag_start(a, h, 0, z, y, dev(z2, y, c))
        ag_start(a, h, 1, z, y, dev(z, yp, c))
        ag_start(a, h, 2, z, y, dev(z, ym, c))
        ag_start(a, h, 9, z, y, sibling)

    def ag_second(a, h):
        ag_wait(a, h, 1, z, ym, c)
        ag_start(a, h, 3, z, ym, dev(z, yp, c), HEAD)
        ag_wait(a, h, 2, z, yp, c)
        ag_start(a, h, 4, z, yp, dev(z, ym, c), TAIL)
        ag_wait(a, h, 0, z2, y, c)
        ag_start(a, h, 5, z2, y, dev(z, yp, c), BUT_LAST)
        ag_start(a, h, 6, z2, y, dev(z, ym, c), BUT_FIRST)
        ag_start(a, h, 19, z, yp, dev(z2, y, c), FIRST)
        ag_start(a, h, 20, z, ym, dev(z2, y, c), LAST)
        ag_start(a, h, 10, z, ym, sibling)
        ag_start(a, h, 11, z, yp, sibling)
        ag_start(a, h, 12, z2, y, sibling)

    def ag_third(a, h):
        ag_wait(a, h, 3, z, y2, c, HEAD)
        ag_start(a, h, 7, z, y2, dev(z2, y, c), HEAD)
        ag_wait(a, h, 4, z, y2, c, TAIL)
        ag_start(a, h, 8, z, y2, dev(z2, y, c), TAIL)
        ag_start(a, h, 13, z, y2, sibling, HEAD)
        ag_start(a, h, 14, z, y2, sibling, TAIL)

    def ag_fourth(a, h):
        ag_wait(a, h, 5, z2, ym, c, BUT_LAST)
        ag_wait(a, h, 20, z2, ym, c, LAST)
        ag_start(a, h, 15, z2, ym, sibling)
        ag_wait(a, h, 6, z2, yp, c, BUT_FIRST)
        ag_wait(a, h, 19, z2, yp, c, FIRST)
        ag_start(a, h, 16, z2, yp, sibling)
        ag_wait(a, h, 7, z2, y2, c, HEAD)
        ag_start(a, h, 17, z2, y2, sibling, HEAD)
        ag_wait(a, h, 8, z2, y2, c, TAIL)
        ag_start(a, h, 18, z2, y2, sibling, TAIL)

    def multiply(a, h, pair, first=False):
        at = pair * (2 * CHIP)
        at = pl.ds(pl.multiple_of(at, 2 * CHIP), 2 * CHIP)
        if a == 0:
            total, term = bh, nn_dot(wd[:, at], g_all[h][at])
        else:
            total, term = pre, tn_dot(wu[at], x_all[h][at])
        total[h][...] = term if first else total[h][...] + term

    here, across = z * 2 + y // 2, z2 * 2 + y // 2
    here_2, across_2 = z * 2 + 1 - y // 2, z2 * 2 + 1 - y // 2

    def mul_1(a, h):
        ag_wait(a, h, 9, z, y, oc)
        ag_wait(a, h, 10, z, ym, oc)
        ag_wait(a, h, 11, z, yp, oc)
        multiply(a, h, here, True)

    def mul_2(a, h):
        ag_wait(a, h, 13, z, y2, oc, HEAD)
        ag_wait(a, h, 14, z, y2, oc, TAIL)
        multiply(a, h, here_2)

    def mul_3(a, h):
        ag_wait(a, h, 12, z2, y, oc)
        ag_wait(a, h, 15, z2, ym, oc)
        ag_wait(a, h, 16, z2, yp, oc)
        multiply(a, h, across)
        ag_wait(a, h, 17, z2, y2, oc, HEAD)
        ag_wait(a, h, 18, z2, y2, oc, TAIL)
        multiply(a, h, across_2)

    def put_row(ref, at, row):
        ref[at : at + 1] = row[:, 0:256]
        ref[at + 1 : at + 2, 0 : row.shape[1] - 256] = row[:, 256:]

    def get_row(ref, at, count):
        return jnp.concatenate([ref[at : at + 1], ref[at + 1 : at + 2, 0 : count - 256]], axis=1)

    own = rows(q_me * CHIP + c * LOCAL, LOCAL)
    load_acts.wait()
    values = acts[...].astype(F32)
    mean_here = jnp.mean(values, axis=0, keepdims=True)
    spread = values - mean_here
    put_row(my_facts, 0, mean_here)
    put_row(my_facts, 2, jnp.sum(spread * spread, axis=0, keepdims=True))
    gain_row = gain_ref[...].astype(F32)
    put_row(my_facts, 4, gain_row)
    send(my_facts, sib_facts, facts_send.at[7], facts_recv.at[7], sibling)
    load_grad.wait()
    for h in range(2):
        token = lax.broadcasted_iota(jnp.int32, (LOCAL, TOKS[h]), 1) + FROM[h]
        alive = (token // MB_TOK < live_ref[0]).astype(F32)
        g_all[h][own] = (grads[:, span(h)].astype(F32) * alive).astype(BF16)
    recv(sib_facts, facts_send.at[7], facts_recv.at[7])
    mean_a, mean_b = my_facts[0:2], sib_facts[0:2]
    mean_chip = 0.5 * (mean_a + mean_b)
    apart_a, apart_b = mean_a - mean_chip, mean_b - mean_chip
    facts[q_me, 0:2] = mean_chip
    facts[q_me, 2:4] = (
        my_facts[2:4] + sib_facts[2:4] + LOCAL * (apart_a * apart_a + apart_b * apart_b)
    )
    facts[q_me, 4:6] = jnp.where(c == 0, my_facts[4:6], sib_facts[4:6])
    facts[q_me, 6:8] = jnp.where(c == 0, sib_facts[4:6], my_facts[4:6])
    for i in range(7):
        send(facts.at[q_me], facts.at[q_me], facts_send.at[i], facts_recv.at[i], mate(i))
    ag_own(0, 0)
    ag_own(0, 1)
    across_eye = lax.broadcasted_iota(jnp.int32, (LOCAL, LOCAL), 0) == lax.broadcasted_iota(
        jnp.int32, (LOCAL, LOCAL), 1
    )
    gain_col = jnp.sum(jnp.where(across_eye, gain_row, 0.0), axis=1, keepdims=True)
    for i in range(7):
        recv(facts.at[mate_from(i)], facts_send.at[i], facts_recv.at[i])
    means = [facts[i, 0:2] for i in range(CHIPS)]
    mean_two = sum(means) / CHIPS
    square_two = sum(facts[i, 2:4] for i in range(CHIPS))
    square_two += CHIP * sum((m - mean_two) * (m - mean_two) for m in means)
    rstd_two = lax.rsqrt(square_two / D + 1e-05)
    mean_row = jnp.concatenate([mean_two[0:1], mean_two[1:2]], axis=1)
    rstd_row = jnp.concatenate([rstd_two[0:1], rstd_two[1:2]], axis=1)
    normed[...] = (acts[...].astype(F32) - mean_row) * rstd_row
    x_all[0][own] = (normed[:, span(0)] * gain_col).astype(BF16)
    ag_own(1, 0)
    x_all[1][own] = (normed[:, span(1)] * gain_col).astype(BF16)

    def row_sums(h):
        def tile(i, second):
            at = rows(i * 128, 128)
            u = pre[h][at]
            slope = (
                0.5 * (1.0 + lax.erf(u * 0.7071067811865476))
                + u * jnp.exp(-0.5 * u * u) * 0.3989422804014327
            )
            b = (bh[h][at] * slope).astype(BF16)
            bp[h][at] = b
            return second + jnp.sum(b.astype(F32) * u, axis=0, keepdims=True)

        second = lax.fori_loop(0, CHIP // 128, tile, jnp.zeros((1, TOKS[h]), F32))
        first = nn_dot(weight_rows[...], bp[h][...])
        sums[h][0:1] = first[0:1] + first[1:2]
        sums[h][1:2] = second
        send(sums[h], sib_sums[h], sums_send.at[h, 7], sums_recv.at[h, 7], sibling)

    def spread_sums(h):
        recv(sib_sums[h], sums_send.at[h, 7], sums_recv.at[h, 7])
        all_sums[h][q_me] = sums[h][...] + sib_sums[h][...]
        mine = all_sums[h].at[q_me]
        for i in range(7):
            send(mine, mine, sums_send.at[h, i], sums_recv.at[h, i], mate(i))

    def chip(zz, yy):
        return zz * 4 + yy

    def mine_of(h, q, half=None):
        first, count = (0, LOCAL) if half is None else half
        return part[h].at[rows(q * CHIP + c * LOCAL + first, count)]

    def cut(ref, at):
        return ref.at[pl.ds(*at)]

    q_p, q_m, q_2 = chip(z, yp), chip(z, ym), chip(z, y2)
    q_z, q_zp, q_zm, q_z2 = chip(z2, y), chip(z2, yp), chip(z2, ym), chip(z2, y2)

    def sib_copy(h, q):
        return remote(
            part[h].at[rows(q * CHIP + oc * LOCAL, LOCAL)], sib_part[h].at[q],
            sib_send.at[h, q], sib_recv.at[h, q], sibling,
        )

    def rs_copy(h, tag, src, dst, where):
        return remote(src, dst, rs_send.at[h, tag], rs_recv.at[h, tag], where)

    def rs_start(h, tag, src, dst, where):
        copy = rs_copy(h, tag, src, dst, where)
        copy.start()
        sends.append(copy)

    def rs_wait(h, tag, dst):
        recv(dst, rs_send.at[h, tag], rs_recv.at[h, tag])

    def add(ref, *others):
        total = ref[...].astype(F32)
        for other in others:
            total += other[...].astype(F32)
        ref[...] = total.astype(BF16)

    def rs_first(h):
        def put(tag, q, at, dst, where):
            return lambda: rs_copy(h, tag, mine_of(h, q, at), dst, where)

        across, up, down = dev(z2, y, c), dev(z, yp, c), dev(z, ym, c)
        early = [
            [put(0, q_z2, None, r_a[h], across)],
            [
                put(1, q_zp, BUT_FIRST, cut(r_b[h].at[0], BUT_FIRST), up),
                put(10, q_zp, FIRST, r_p[h].at[0], across),
            ],
            [
                put(2, q_zm, BUT_LAST, cut(r_b[h].at[1], BUT_LAST), down),
                put(11, q_zm, LAST, r_p[h].at[1], across),
            ],
            [put(3, q_p, TAIL, cut(r_e[h].at[0], TAIL), up)],
            [put(4, q_m, HEAD, cut(r_e[h].at[1], HEAD), down)],
        ]

        def chip_at(k):
            dz = pick([t[0] for t in SUM_ORDER], k)
            dy = pick([t[1] for t in SUM_ORDER], k)
            return chip((z + dz) % 2, (y + dy) % 4)

        def product(k):
            q = chip_at(k)
            at = pl.ds(pl.multiple_of(q * CHIP, CHIP), CHIP)
            part[h][at] = nn_dot(wu[at], bp[h][...]).astype(BF16)
            sib_copy(h, q).start()

        def join(k):
            q = chip_at(k)
            sib_copy(h, q).wait_recv()
            add(mine_of(h, q), sib_part[h].at[q])

        @pl.loop(0, LAG)
        def _(k):
            product(k)

        @pl.loop(LAG, CHIPS)
        def _(k):
            product(k)
            join(k - LAG)
            for i, makes in enumerate(early):

                @pl.when(k == LAG + i)
                def _(makes=makes):
                    for make in makes:
                        make().start()

        @pl.loop(CHIPS - LAG, CHIPS)
        def _(k):
            join(k)

        for makes in early:
            sends.extend(make() for make in makes)

    def rs_second(h):
        rs_wait(h, 0, r_a[h])
        add(mine_of(h, q_2), r_a[h])
        rs_start(h, 5, mine_of(h, q_2, HEAD), r_c[h].at[0], dev(z, yp, c))
        rs_start(h, 6, mine_of(h, q_2, TAIL), r_c[h].at[1], dev(z, ym, c))
        rs_wait(h, 1, cut(r_b[h].at[0], BUT_FIRST))
        rs_wait(h, 2, cut(r_b[h].at[1], BUT_LAST))
        add(mine_of(h, q_z, BUT_FIRST), cut(r_b[h].at[0], BUT_FIRST))
        add(mine_of(h, q_z, BUT_LAST), cut(r_b[h].at[1], BUT_LAST))
        rs_start(h, 7, mine_of(h, q_z), r_d[h], dev(z2, y, c))
        rs_wait(h, 10, r_p[h].at[0])
        add(mine_of(h, q_p, FIRST), r_p[h].at[0])
        rs_wait(h, 11, r_p[h].at[1])
        add(mine_of(h, q_m, LAST), r_p[h].at[1])

    def rs_third(h):
        rs_wait(h, 5, r_c[h].at[0])
        add(mine_of(h, q_p, HEAD), r_c[h].at[0])
        rs_start(h, 8, mine_of(h, q_p, HEAD), cut(r_e[h].at[0], HEAD), dev(z, yp, c))
        rs_wait(h, 6, r_c[h].at[1])
        add(mine_of(h, q_m, TAIL), r_c[h].at[1])
        rs_start(h, 9, mine_of(h, q_m, TAIL), cut(r_e[h].at[1], TAIL), dev(z, ym, c))

    def move_copy(h):
        return remote(
            out_buf[h], moved[h].at[rows(c * LOCAL, LOCAL)], move_send.at[h, 0],
            move_recv.at[h, 0], ((s + sections - 1) % sections, p),
        )

    def finish(h):
        for i in range(7):
            recv(all_sums[h].at[mate_from(i)], sums_send.at[h, i], sums_recv.at[h, i])
        totals = sum(all_sums[h][i] for i in range(CHIPS)) / D
        rs_wait(h, 7, r_d[h])
        rs_wait(h, 3, cut(r_e[h].at[0], TAIL))
        rs_wait(h, 4, cut(r_e[h].at[1], HEAD))
        rs_wait(h, 8, cut(r_e[h].at[0], HEAD))
        rs_wait(h, 9, cut(r_e[h].at[1], TAIL))
        summed = (
            mine_of(h, q_me)[...].astype(F32)
            + r_d[h][...].astype(F32)
            + r_e[h][0].astype(F32)
            + r_e[h][1].astype(F32)
        )
        at = span(h)
        back = summed * gain_col - totals[0:1] - normed[:, at] * totals[1:2]
        total = rstd_row[:, at] * back + g_all[h][own].astype(F32)
        out_buf[h][...] = total.astype(BF16)

        @pl.when(s > 0)
        def _():
            move_copy(h).start()

    def move_second(h):
        there = moved[h].at[rows(c * LOCAL, LOCAL)]

        @pl.when(s < sections - 1)
        def _():
            recv(there, move_send.at[h, 0], move_recv.at[h, 0])

        @pl.when(s == sections - 1)
        def _():
            there[...] = jnp.zeros((LOCAL, TOKS[h]), BF16)

        send(there, there, move_send.at[h, 1], move_recv.at[h, 1], sibling)

    def place_rows(h):
        recv(moved[h].at[rows(oc * LOCAL, LOCAL)], move_send.at[h, 1], move_recv.at[h, 1])
        return nt_dot(chosen[:, span(h)], moved[h][...])

    count = live_ref[0].astype(F32)

    def grad_up(k):
        at = pl.ds(k * GU, GU)
        term = nt_dot(x_all[0][at], bp[0][...]) + nt_dot(x_all[1][at], bp[1][...])
        gu_ref[at] = (term / count).astype(BF16)

    ag_second(0, 0)
    load_wd.wait()
    ag_second(1, 0)
    ag_own(1, 1)
    ag_second(0, 1)
    mul_1(0, 0)
    load_wu.wait()
    mul_1(1, 0)
    ag_third(0, 0)
    ag_third(1, 0)
    weights = jnp.zeros((16, CHIP), F32)
    for i in range(CHIPS):
        for j in range(2):
            gain_ij = get_row(facts.at[i], 4 + 2 * j, LOCAL)
            gain_ij = jnp.broadcast_to(gain_ij, (16, LOCAL)).astype(BF16)
            at = i * CHIP + j * LOCAL
            weights += nn_dot(gain_ij, wu[at : at + LOCAL])
    high = weights.astype(BF16).astype(F32)
    line = lax.broadcasted_iota(jnp.int32, (16, CHIP), 0)
    weight_rows[...] = jnp.where(
        line == 0, high, jnp.where(line == 1, weights - high, 0.0)
    ).astype(BF16)
    mul_2(0, 0)
    mul_2(1, 0)
    ag_second(1, 1)
    ag_fourth(0, 0)
    mul_3(0, 0)
    ag_fourth(1, 0)
    ag_third(0, 1)
    mul_3(1, 0)
    row_sums(0)
    rs_first(0)
    spread_sums(0)
    ag_third(1, 1)
    mul_1(0, 1)
    mul_1(1, 1)
    rs_second(0)
    ag_fourth(0, 1)
    mul_2(0, 1)
    mul_2(1, 1)
    mul_3(0, 1)
    rs_third(0)
    ag_fourth(1, 1)
    mul_3(1, 1)
    row_sums(1)
    rs_first(1)
    spread_sums(1)
    finish(0)

    base = jnp.minimum(s + 1, sections - 1) * MB
    names = [senders_ref[base + m] for m in range(MB)]
    token = lax.broadcasted_iota(jnp.int32, (SLOT, ROWS), 1)
    slot_row = token % MB_TOK
    for m in range(MB):
        rank = jnp.int32(0)
        for before in range(m):
            rank = rank + jnp.where(names[before] == names[m], 1, 0)
        slot_row += jnp.where(token // MB_TOK == m, (names[m] * 2 + rank) * MB_TOK, 0)
    row = lax.broadcasted_iota(jnp.int32, (SLOT, ROWS), 0)
    for i, (dz, dy) in enumerate(MATES + [(0, 0)]):
        peer = chip((z + dz) % 2, (y + dy) % 4) * 2 + c
        chosen[i * SLOT : (i + 1) * SLOT] = jnp.where(
            slot_row == row + peer * SLOT, 1.0, 0.0
        ).astype(BF16)

    grad_up(0)
    rs_second(1)
    move_second(0)
    grad_up(1)
    rs_third(1)
    routed[...] = place_rows(0)
    grad_up(2)
    grad_up(3)
    finish(1)
    move_second(1)
    routed[...] += place_rows(1)
    columns = pl.ds(pl.multiple_of(q_me * CHIP, CHIP), CHIP)
    for i in range(7):
        stage[i] = routed[i * SLOT : (i + 1) * SLOT].astype(BF16)
        send(stage.at[i], landed.at[:, columns], put_send.at[i], put_recv.at[i], mate(i))
    landed[:, columns] = routed[7 * SLOT :].astype(BF16)
    for i in range(7):
        there = landed.at[:, pl.ds(pl.multiple_of(mate_from(i) * CHIP, CHIP), CHIP)]
        recv(there, put_send.at[i], put_recv.at[i])
    returned_ref[...] = landed[...]

    for h in range(2):

        @pl.loop(0, CHIPS)
        def _(k):
            sib_copy(h, k).wait_send()

        @pl.when(s > 0)
        def _():
            move_copy(h).wait_send()

    for copy in sends:
        copy.wait_send()


def both(make):
    return tuple(make(t) for t in TOKS)


def layer(acts, grad_out, gain, live, senders, w_up, w_down):
    vmem, anyspace = pl.BlockSpec(memory_space=pltpu.VMEM), pl.BlockSpec(memory_space=pl.ANY)
    smem = pl.BlockSpec(memory_space=pltpu.SMEM)
    dma = pltpu.SemaphoreType.DMA
    return pl.pallas_call(
        layer_kernel,
        out_shape=[
            pltpu.VMEM((D, CHIP), BF16),
            pltpu.VMEM((SLOT, D), BF16),
        ],
        in_specs=[anyspace, anyspace, vmem, smem, smem, anyspace, anyspace],
        out_specs=[vmem, vmem],
        scratch_shapes=[
            pltpu.VMEM((D, CHIP), BF16),
            pltpu.VMEM((CHIP, D), BF16),
            both(lambda t: pltpu.VMEM((D, t), BF16)),
            both(lambda t: pltpu.VMEM((D, t), BF16)),
            both(lambda t: pltpu.VMEM((CHIP, t), F32)),
            both(lambda t: pltpu.VMEM((CHIP, t), F32)),
            both(lambda t: pltpu.VMEM((CHIP, t), BF16)),
            both(lambda t: pltpu.VMEM((D, t), BF16)),
            both(lambda t: pltpu.VMEM((CHIPS, LOCAL, t), BF16)),
            both(lambda t: pltpu.VMEM((LOCAL, t), BF16)),
            both(lambda t: pltpu.VMEM((2, LOCAL, t), BF16)),
            both(lambda t: pltpu.VMEM((2, PART, t), BF16)),
            both(lambda t: pltpu.VMEM((2, LOCAL, t), BF16)),
            both(lambda t: pltpu.VMEM((LOCAL, t), BF16)),
            both(lambda t: pltpu.VMEM((2, PIECE, t), BF16)),
            pltpu.VMEM((LOCAL, ROWS), BF16),
            pltpu.VMEM((LOCAL, ROWS), BF16),
            pltpu.VMEM((LOCAL, ROWS), F32),
            pltpu.VMEM((CHIPS, 8, 256), F32),
            pltpu.VMEM((8, 256), F32),
            pltpu.VMEM((8, 256), F32),
            both(lambda t: pltpu.VMEM((8, t), F32)),
            both(lambda t: pltpu.VMEM((8, t), F32)),
            both(lambda t: pltpu.VMEM((CHIPS, 8, t), F32)),
            pltpu.VMEM((16, CHIP), BF16),
            both(lambda t: pltpu.VMEM((LOCAL, t), BF16)),
            both(lambda t: pltpu.VMEM((CHIP, t), BF16)),
            pltpu.VMEM((CHIPS * SLOT, ROWS), BF16),
            pltpu.VMEM((CHIPS * SLOT, CHIP), F32),
            pltpu.VMEM((7, SLOT, CHIP), BF16),
            pltpu.VMEM((SLOT, D), BF16),
            dma((4, N_AG)),
            dma((4, N_AG)),
            dma((8,)),
            dma((8,)),
            dma((2, 8)),
            dma((2, 8)),
            dma((2, CHIPS)),
            dma((2, CHIPS)),
            dma((2, N_RS)),
            dma((2, N_RS)),
            dma((2, 2)),
            dma((2, 2)),
            dma((7,)),
            dma((7,)),
            dma((4,)),
        ],
        compiler_params=pltpu.CompilerParams(
            collective_id=0, has_side_effects=True, vmem_limit_bytes=48 * MIB
        ),
        cost_estimate=pl.CostEstimate(
            flops=8 * ROWS * D * CHIP, bytes_accessed=20 * MIB, transcendentals=2 * ROWS * CHIP
        ),
    )(acts, grad_out, gain, live, senders, w_up, w_down)


def body(acts, grad_out, gain, w_up, w_down, senders, live):
    grad_up, returned = layer(acts.T, grad_out.T, gain, live, senders[:, 0], w_up, w_down)
    return (grad_up[None], returned)


def solution(mesh):
    in_specs = (
        P("section", "peer"),
        P("section", "peer"),
        P("section", "peer"),
        P("section", None, "peer"),
        P("section", "peer", None),
        P(),
        P("section"),
    )
    out_specs = (P("section", None, "peer"), P(("section", "peer"), None))
    return jax.shard_map(body, mesh=mesh, in_specs=in_specs, out_specs=out_specs, check_vma=False)
```

```python
import jax
import jax.numpy as jnp
from jax import lax
from jax.experimental import pallas as pl
from jax.experimental.pallas import tpu as pltpu
from jax.sharding import PartitionSpec as P

MESH = pl.DeviceIdType.MESH
F32 = jnp.float32
BF16 = jnp.bfloat16
MB = 16
MB_TOK = 32
ROWS = 512
TOKS = (256, 256)
FROM = (0, 256)
D = 5120
CHIP = 640
LOCAL = 320
PART = 160
CHIPS = 8
SLOT = 2 * MB_TOK
PIECE = 48
HEAD, TAIL = (0, PART), (PART, PART)
FIRST, BUT_FIRST = (0, PIECE), (PIECE, LOCAL - PIECE)
LAST, BUT_LAST = (LOCAL - PIECE, PIECE), (0, LOCAL - PIECE)
PARTS = (((LOCAL, PIECE),), ((LOCAL, PIECE),))
WIDTHS = (128, 128, 64)
GU = 1280
MIB = 2**20

MATES = [(0, 1), (0, 2), (0, 3), (1, 0), (1, 1), (1, 2), (1, 3)]
SUM_ORDER = [(1, 2), (1, 1), (1, 3), (0, 1), (0, 3), (0, 2), (1, 0), (0, 0)]
LAG = 3
N_AG = 21
N_RS = 12


def nn_dot(a, b):
    return jnp.dot(a, b, preferred_element_type=F32)


def nt_dot(a, b):
    return lax.dot_general(a, b, (((1,), (1,)), ((), ())), preferred_element_type=F32)


def tn_dot(a, b):
    return lax.dot_general(a, b, (((0,), (0,)), ((), ())), preferred_element_type=F32)


def span(h):
    return slice(FROM[h], FROM[h] + TOKS[h])


def pick(table, k):
    out = table[0]
    for i in range(1, len(table)):
        out = jnp.where(k == i, table[i], out)
    return out


def layer_kernel(
    acts_hbm, grad_hbm, gain_ref, live_ref, senders_ref, wu_hbm, wd_hbm,
    gu_ref, returned_ref,
    wu, wd, g_all, x_all, pre, bh, bp, part, sib_part, r_a, r_b, r_c, r_e, r_d, r_p,
    acts, grads, normed, facts, my_facts, sib_facts, sums, sib_sums, all_sums, weight_rows,
    gain_rows, out_buf, moved, chosen, routed, stage, landed,
    ag_send, ag_recv, facts_send, facts_recv, sums_send, sums_recv,
    sib_send, sib_recv, rs_send, rs_recv, move_send, move_recv, put_send, put_recv,
    local_sem,
):
    s, p = lax.axis_index("section"), lax.axis_index("peer")
    q_me, c = p // 2, p % 2
    z, y, oc = q_me // 4, q_me % 4, 1 - c
    z2, yp, ym, y2 = 1 - z, (y + 1) % 4, (y + 3) % 4, (y + 2) % 4
    sections = lax.axis_size("section")

    def dev(zz, yy, cc):
        return (s, (zz * 4 + yy) * 2 + cc)

    def mate(i):
        dz, dy = MATES[i]
        return dev((z + dz) % 2, (y + dy) % 4, c)

    def mate_from(i):
        dz, dy = MATES[i]
        return ((z + dz) % 2) * 4 + (y + 4 - dy) % 4

    sibling = dev(z, y, oc)
    sends = []

    def remote(src, dst, ssem, rsem, where):
        return pltpu.make_async_remote_copy(
            src_ref=src, dst_ref=dst, send_sem=ssem, recv_sem=rsem,
            device_id=where, device_id_type=MESH,
        )

    def send(src, dst, ssem, rsem, where):
        copy = remote(src, dst, ssem, rsem, where)
        copy.start()
        sends.append(copy)

    def recv(dst, ssem, rsem):
        remote(dst, dst, ssem, rsem, sibling).wait_recv()

    def rows(at, count):
        return pl.ds(pl.multiple_of(at, 16), count)

    load_grad = pltpu.make_async_copy(grad_hbm, grads, local_sem.at[0])
    load_acts = pltpu.make_async_copy(acts_hbm, acts, local_sem.at[1])
    load_wd = pltpu.make_async_copy(wd_hbm.at[0], wd, local_sem.at[2])
    load_wu = pltpu.make_async_copy(wu_hbm.at[0], wu, local_sem.at[3])
    load_grad.start()
    load_acts.start()
    load_wd.start()
    load_wu.start()

    barrier = pltpu.get_barrier_semaphore()
    pl.semaphore_signal(barrier, inc=1, device_id=sibling, device_id_type=MESH)
    for i in range(7):
        pl.semaphore_signal(barrier, inc=1, device_id=mate(i), device_id_type=MESH)
    for step in (1, sections - 1):
        pl.semaphore_signal(
            barrier, inc=1, device_id=((s + step) % sections, p), device_id_type=MESH
        )
    pl.semaphore_wait(barrier, 10)

    bufs = (g_all, x_all)

    def block(a, h, zz, yy, cc, half=None):
        at = (zz * 4 + yy) * CHIP + cc * LOCAL
        first, count = (0, LOCAL) if half is None else half
        return bufs[a][h].at[rows(at + first, count)]

    def ag_start(a, h, tag, zz, yy, where, half=None):
        ref = block(a, h, zz, yy, c, half)
        send(ref, ref, ag_send.at[2 * a + h, tag], ag_recv.at[2 * a + h, tag], where)

    def ag_wait(a, h, tag, zz, yy, cc, half=None):
        recv(block(a, h, zz, yy, cc, half), ag_send.at[2 * a + h, tag], ag_recv.at[2 * a + h, tag])

    def ag_own(a, h):
        ag_start(a, h, 0, z, y, dev(z2, y, c))
        ag_start(a, h, 1, z, y, dev(z, yp, c))
        ag_start(a, h, 2, z, y, dev(z, ym, c))
        ag_start(a, h, 9, z, y, sibling)

    def ag_halves(a, h):
        ag_wait(a, h, 1, z, ym, c)
        ag_start(a, h, 3, z, ym, dev(z, yp, c), HEAD)
        ag_wait(a, h, 2, z, yp, c)
        ag_start(a, h, 4, z, yp, dev(z, ym, c), TAIL)
        ag_start(a, h, 19, z, yp, dev(z2, y, c), FIRST)
        ag_start(a, h, 20, z, ym, dev(z2, y, c), LAST)
        ag_start(a, h, 10, z, ym, sibling)
        ag_start(a, h, 11, z, yp, sibling)

    def ag_across(a, h):
        ag_wait(a, h, 0, z2, y, c)
        ag_start(a, h, 5, z2, y, dev(z, yp, c), BUT_LAST)
        ag_start(a, h, 6, z2, y, dev(z, ym, c), BUT_FIRST)
        ag_start(a, h, 12, z2, y, sibling)

    def ag_third(a, h):
        ag_wait(a, h, 3, z, y2, c, HEAD)
        ag_start(a, h, 7, z, y2, dev(z2, y, c), HEAD)
        ag_wait(a, h, 4, z, y2, c, TAIL)
        ag_start(a, h, 8, z, y2, dev(z2, y, c), TAIL)
        ag_start(a, h, 13, z, y2, sibling, HEAD)
        ag_start(a, h, 14, z, y2, sibling, TAIL)

    def ag_fourth(a, h):
        ag_wait(a, h, 5, z2, ym, c, BUT_LAST)
        ag_wait(a, h, 20, z2, ym, c, LAST)
        ag_start(a, h, 15, z2, ym, sibling)
        ag_wait(a, h, 6, z2, yp, c, BUT_FIRST)
        ag_wait(a, h, 19, z2, yp, c, FIRST)
        ag_start(a, h, 16, z2, yp, sibling)
        ag_wait(a, h, 7, z2, y2, c, HEAD)
        ag_start(a, h, 17, z2, y2, sibling, HEAD)
        ag_wait(a, h, 8, z2, y2, c, TAIL)
        ag_start(a, h, 18, z2, y2, sibling, TAIL)

    def multiply(a, h, pair, first=False):
        at = pair * (2 * CHIP)
        at = pl.ds(pl.multiple_of(at, 2 * CHIP), 2 * CHIP)
        if a == 0:
            total, term = bh, nn_dot(wd[:, at], g_all[h][at])
        else:
            total, term = pre, tn_dot(wu[at], x_all[h][at])
        total[h][...] = term if first else total[h][...] + term

    here, across = z * 2 + y // 2, z2 * 2 + y // 2
    here_2, across_2 = z * 2 + 1 - y // 2, z2 * 2 + 1 - y // 2

    def mul_1(a, h):
        ag_wait(a, h, 9, z, y, oc)
        ag_wait(a, h, 10, z, ym, oc)
        ag_wait(a, h, 11, z, yp, oc)
        multiply(a, h, here, True)

    def mul_2(a, h):
        ag_wait(a, h, 13, z, y2, oc, HEAD)
        ag_wait(a, h, 14, z, y2, oc, TAIL)
        multiply(a, h, here_2)

    def mul_3(a, h):
        ag_wait(a, h, 12, z2, y, oc)
        ag_wait(a, h, 15, z2, ym, oc)
        ag_wait(a, h, 16, z2, yp, oc)
        multiply(a, h, across)
        ag_wait(a, h, 17, z2, y2, oc, HEAD)
        ag_wait(a, h, 18, z2, y2, oc, TAIL)
        multiply(a, h, across_2)

    def put_row(ref, at, row):
        ref[at : at + 1] = row[:, 0:256]
        ref[at + 1 : at + 2, 0 : row.shape[1] - 256] = row[:, 256:]

    def get_row(ref, at, count):
        return jnp.concatenate([ref[at : at + 1], ref[at + 1 : at + 2, 0 : count - 256]], axis=1)

    own = rows(q_me * CHIP + c * LOCAL, LOCAL)
    load_grad.wait()
    for h in range(2):
        token = lax.broadcasted_iota(jnp.int32, (LOCAL, TOKS[h]), 1) + FROM[h]
        alive = (token // MB_TOK < live_ref[0]).astype(F32)
        g_all[h][own] = (grads[:, span(h)].astype(F32) * alive).astype(BF16)
    ag_own(0, 0)
    load_acts.wait()
    values = acts[...].astype(F32)
    mean_here = jnp.mean(values, axis=0, keepdims=True)
    spread = values - mean_here
    put_row(my_facts, 0, mean_here)
    put_row(my_facts, 2, jnp.sum(spread * spread, axis=0, keepdims=True))
    gain_row = gain_ref[...].astype(F32)
    put_row(my_facts, 4, gain_row)
    send(my_facts, sib_facts, facts_send.at[7], facts_recv.at[7], sibling)
    recv(sib_facts, facts_send.at[7], facts_recv.at[7])
    mean_a, mean_b = my_facts[0:2], sib_facts[0:2]
    mean_chip = 0.5 * (mean_a + mean_b)
    apart_a, apart_b = mean_a - mean_chip, mean_b - mean_chip
    facts[q_me, 0:2] = mean_chip
    facts[q_me, 2:4] = (
        my_facts[2:4] + sib_facts[2:4] + LOCAL * (apart_a * apart_a + apart_b * apart_b)
    )
    facts[q_me, 4:6] = jnp.where(c == 0, my_facts[4:6], sib_facts[4:6])
    facts[q_me, 6:8] = jnp.where(c == 0, sib_facts[4:6], my_facts[4:6])
    for i in range(7):
        send(facts.at[q_me], facts.at[q_me], facts_send.at[i], facts_recv.at[i], mate(i))
    ag_own(0, 1)
    across_eye = lax.broadcasted_iota(jnp.int32, (LOCAL, LOCAL), 0) == lax.broadcasted_iota(
        jnp.int32, (LOCAL, LOCAL), 1
    )
    gain_col = jnp.sum(jnp.where(across_eye, gain_row, 0.0), axis=1, keepdims=True)
    gain_rows[...] = jnp.broadcast_to(gain_col, (LOCAL, 128))
    for i in range(7):
        recv(facts.at[mate_from(i)], facts_send.at[i], facts_recv.at[i])
    means = [facts[i, 0:2] for i in range(CHIPS)]
    mean_two = sum(means) / CHIPS
    square_two = sum(facts[i, 2:4] for i in range(CHIPS))
    square_two += CHIP * sum((m - mean_two) * (m - mean_two) for m in means)
    rstd_two = lax.rsqrt(square_two / D + 1e-05)
    mean_row = jnp.concatenate([mean_two[0:1], mean_two[1:2]], axis=1)
    rstd_row = jnp.concatenate([rstd_two[0:1], rstd_two[1:2]], axis=1)
    normed[...] = (acts[...].astype(F32) - mean_row) * rstd_row
    for h in range(2):
        x_all[h][own] = (normed[:, span(h)] * gain_col).astype(BF16)
        ag_own(1, h)

    def row_sums(h):
        def tile(i, second):
            at = rows(i * 128, 128)
            u = pre[h][at]
            slope = (
                0.5 * (1.0 + lax.erf(u * 0.7071067811865476))
                + u * jnp.exp(-0.5 * u * u) * 0.3989422804014327
            )
            b = (bh[h][at] * slope).astype(BF16)
            bp[h][at] = b
            return second + jnp.sum(b.astype(F32) * u, axis=0, keepdims=True)

        second = lax.fori_loop(0, CHIP // 128, tile, jnp.zeros((1, TOKS[h]), F32))
        first = nn_dot(weight_rows[...], bp[h][...])
        sums[h][0:1] = first[0:1] + first[1:2]
        sums[h][1:2] = second
        send(sums[h], sib_sums[h], sums_send.at[h, 7], sums_recv.at[h, 7], sibling)

    def spread_sums(h):
        recv(sib_sums[h], sums_send.at[h, 7], sums_recv.at[h, 7])
        all_sums[h][q_me] = sums[h][...] + sib_sums[h][...]
        mine = all_sums[h].at[q_me]
        for i in range(7):
            send(mine, mine, sums_send.at[h, i], sums_recv.at[h, i], mate(i))

    def chip(zz, yy):
        return zz * 4 + yy

    def offset(j):
        return (c * 192, 128 - c * 64, (1 - c) * 256)[j]

    def part_rows(h, j):
        count, over = PARTS[h][j]
        first = offset(j) if len(PARTS[h]) > 1 else 0
        half = count // 2
        return dict(
            all=(first, count),
            head=(first, half),
            tail=(first + half, half),
            first=(first, over),
            but_first=(first + over, count - over),
            last=(first + count - over, over),
            but_last=(first, count - over),
        )

    def mine_of(h, q, at):
        first, count = at
        return part[h].at[rows(q * CHIP + c * LOCAL + first, count)]

    def cut(ref, at):
        first, count = at
        return ref.at[rows(first, count)]

    q_p, q_m, q_2 = chip(z, yp), chip(z, ym), chip(z, y2)
    q_z, q_zp, q_zm, q_z2 = chip(z2, y), chip(z2, yp), chip(z2, ym), chip(z2, y2)

    def sib_copy(h, q):
        return remote(
            part[h].at[rows(q * CHIP + oc * LOCAL, LOCAL)], sib_part[h].at[q],
            sib_send.at[h, q], sib_recv.at[h, q], sibling,
        )

    def rs_copy(h, tag, src, dst, where):
        return remote(src, dst, rs_send.at[tag], rs_recv.at[tag], where)

    def rs_start(h, tag, src, dst, where):
        copy = rs_copy(h, tag, src, dst, where)
        copy.start()
        sends.append(copy)

    def rs_wait(h, tag, dst):
        recv(dst, rs_send.at[tag], rs_recv.at[tag])

    def add(ref, *others):
        total = ref[...].astype(F32)
        for other in others:
            total += other[...].astype(F32)
        ref[...] = total.astype(BF16)

    def tags(h, j):
        return (h * len(PARTS[0]) + j) * N_RS

    def rs_first(h):
        across, up, down = dev(z2, y, c), dev(z, yp, c), dev(z, ym, c)

        def puts(j):
            t, at = tags(h, j), part_rows(h, j)

            def put(tag, q, where, dst, to):
                return lambda: rs_copy(h, t + tag, mine_of(h, q, at[where]), cut(dst, at[where]), to)

            return [
                [put(0, q_z2, "all", r_a[h], across)],
                [
                    put(1, q_zp, "but_first", r_b[h].at[0], up),
                    put(10, q_zp, "first", r_p[h].at[0], across),
                ],
                [
                    put(2, q_zm, "but_last", r_b[h].at[1], down),
                    put(11, q_zm, "last", r_p[h].at[1], across),
                ],
                [put(3, q_p, "tail", r_e[h].at[0], up)],
                [put(4, q_m, "head", r_e[h].at[1], down)],
            ]

        early = [puts(j) for j in range(len(PARTS[h]))]

        def chip_at(k):
            dz = pick([t[0] for t in SUM_ORDER], k)
            dy = pick([t[1] for t in SUM_ORDER], k)
            return chip((z + dz) % 2, (y + dy) % 4)

        def product(k):
            q = chip_at(k)
            at = pl.ds(pl.multiple_of(q * CHIP, CHIP), CHIP)
            part[h][at] = nn_dot(wu[at], bp[h][...]).astype(BF16)
            sib_copy(h, q).start()

        def join(k):
            q = chip_at(k)
            sib_copy(h, q).wait_recv()
            add(mine_of(h, q, (0, LOCAL)), sib_part[h].at[q])

        @pl.loop(0, LAG)
        def _(k):
            product(k)

        @pl.loop(LAG, CHIPS)
        def _(k):
            product(k)
            join(k - LAG)
            for i, makes in enumerate(early[0]):

                @pl.when(k == LAG + i)
                def _(makes=makes):
                    for make in makes:
                        make().start()

        @pl.loop(CHIPS - LAG, CHIPS)
        def _(k):
            join(k)

        for j, groups in enumerate(early):
            for make in [m for group in groups for m in group]:
                copy = make()
                if j > 0:
                    copy.start()
                sends.append(copy)

    def rs_second(h, j=0):
        t, at = tags(h, j), part_rows(h, j)
        rs_wait(h, t, cut(r_a[h], at["all"]))
        add(mine_of(h, q_2, at["all"]), cut(r_a[h], at["all"]))
        head, tail = at["head"], at["tail"]
        rs_start(h, t + 5, mine_of(h, q_2, head), cut(r_c[h].at[0], head), dev(z, yp, c))
        rs_start(h, t + 6, mine_of(h, q_2, tail), cut(r_c[h].at[1], tail), dev(z, ym, c))
        from_m, from_p = cut(r_b[h].at[0], at["but_first"]), cut(r_b[h].at[1], at["but_last"])
        rs_wait(h, t + 1, from_m)
        rs_wait(h, t + 2, from_p)
        add(mine_of(h, q_z, at["but_first"]), from_m)
        add(mine_of(h, q_z, at["but_last"]), from_p)
        rs_start(
            h, t + 7, mine_of(h, q_z, at["all"]), cut(r_d[h], at["all"]), dev(z2, y, c)
        )
        for tag, q, i, where in ((10, q_p, 0, "first"), (11, q_m, 1, "last")):
            there = cut(r_p[h].at[i], at[where])
            rs_wait(h, t + tag, there)
            add(mine_of(h, q, at[where]), there)

    def rs_third(h, j=0):
        t, at = tags(h, j), part_rows(h, j)
        for tag, q, i, where, to in (
            (0, q_p, 0, "head", dev(z, yp, c)),
            (1, q_m, 1, "tail", dev(z, ym, c)),
        ):
            there = cut(r_c[h].at[i], at[where])
            rs_wait(h, t + 5 + tag, there)
            add(mine_of(h, q, at[where]), there)
            rs_start(h, t + 8 + tag, mine_of(h, q, at[where]), cut(r_e[h].at[i], at[where]), to)

    starts = [2 * sum(WIDTHS[:j]) for j in range(3)]

    def place_of(h, j, core):
        return moved[h].at[rows(starts[j] + core * WIDTHS[j], WIDTHS[j])]

    def move_copy(h, j):
        return remote(
            out_buf[h].at[rows(offset(j), WIDTHS[j])], place_of(h, j, c), move_send.at[h, j],
            move_recv.at[h, j], ((s + sections - 1) % sections, p),
        )

    def totals_of(h):
        for i in range(7):
            recv(all_sums[h].at[mate_from(i)], sums_send.at[h, i], sums_recv.at[h, i])
        return sum(all_sums[h][i] for i in range(CHIPS)) / D

    def finish(h, totals, j=0):
        t, at = tags(h, j), part_rows(h, j)
        mine = at["all"]
        rs_wait(h, t + 7, cut(r_d[h], mine))
        rs_wait(h, t + 3, cut(r_e[h].at[0], at["tail"]))
        rs_wait(h, t + 4, cut(r_e[h].at[1], at["head"]))
        rs_wait(h, t + 8, cut(r_e[h].at[0], at["head"]))
        rs_wait(h, t + 9, cut(r_e[h].at[1], at["tail"]))
        summed = mine_of(h, q_me, mine)[...].astype(F32)
        for ref in (r_d[h], r_e[h].at[0], r_e[h].at[1]):
            summed += cut(ref, mine)[...].astype(F32)
        here = rows(*mine)
        gain_here = gain_rows[here, 0:1]
        back = summed * gain_here - totals[0:1] - normed[here, span(h)] * totals[1:2]
        grad_here = g_all[h][rows(q_me * CHIP + c * LOCAL + mine[0], mine[1])].astype(F32)
        out_buf[h][here] = (rstd_row[:, span(h)] * back + grad_here).astype(BF16)

        @pl.when(s > 0)
        def _():
            for i in range(3) if len(PARTS[h]) == 1 else (j,):
                move_copy(h, i).start()

    def move_second(h, j):
        there = place_of(h, j, c)

        @pl.when(s < sections - 1)
        def _():
            recv(there, move_send.at[h, j], move_recv.at[h, j])

        @pl.when(s == sections - 1)
        def _():
            there[...] = jnp.zeros((WIDTHS[j], TOKS[h]), BF16)

        send(there, there, move_send.at[h, 3 + j], move_recv.at[h, 3 + j], sibling)

    def place_rows(h, j):
        recv(place_of(h, j, oc), move_send.at[h, 3 + j], move_recv.at[h, 3 + j])
        features = moved[h][starts[j] : starts[j] + 2 * WIDTHS[j]]
        return nt_dot(chosen[:, span(h)], features)

    COLUMNS = (((0, 128, 0), (512, 128, 128)), ((128, 128, 0), (384, 128, 128)), ((256, 128, 0),))

    def part_columns(q, at, width):
        return pl.ds(pl.multiple_of(q * CHIP + at, 128), width)

    def put_part(j):
        width = 2 * WIDTHS[j]
        both_phases = routed[:, starts[j] : starts[j] + width] + place_rows(1, j)
        stage[j][...] = both_phases.astype(BF16)
        for i in range(7):
            for n, (at, size, source) in enumerate(COLUMNS[j]):
                send(
                    stage[j].at[pl.ds(i * SLOT, SLOT), pl.ds(source, size)],
                    landed.at[:, part_columns(q_me, at, size)],
                    put_send.at[i, 2 * j + n], put_recv.at[i, 2 * j + n], mate(i),
                )
        for at, size, source in COLUMNS[j]:
            landed[:, part_columns(q_me, at, size)] = stage[j][7 * SLOT :, source : source + size]

    def wait_part(j):
        for i in range(7):
            for n, (at, size, _) in enumerate(COLUMNS[j]):
                there = landed.at[:, part_columns(mate_from(i), at, size)]
                recv(there, put_send.at[i, 2 * j + n], put_recv.at[i, 2 * j + n])

    count = live_ref[0].astype(F32)

    def grad_up(k):
        at = pl.ds(k * GU, GU)
        term = nt_dot(x_all[0][at], bp[0][...]) + nt_dot(x_all[1][at], bp[1][...])
        gu_ref[at] = (term / count).astype(BF16)

    ag_halves(0, 0)
    load_wu.wait()
    weights = jnp.zeros((16, CHIP), F32)
    for i in range(CHIPS):
        for j in range(2):
            gain_ij = get_row(facts.at[i], 4 + 2 * j, LOCAL)
            gain_ij = jnp.broadcast_to(gain_ij, (16, LOCAL)).astype(BF16)
            at = i * CHIP + j * LOCAL
            weights += nn_dot(gain_ij, wu[at : at + LOCAL])
    high = weights.astype(BF16).astype(F32)
    line = lax.broadcasted_iota(jnp.int32, (16, CHIP), 0)
    weight_rows[...] = jnp.where(
        line == 0, high, jnp.where(line == 1, weights - high, 0.0)
    ).astype(BF16)
    base = jnp.minimum(s + 1, sections - 1) * MB
    names = [senders_ref[base + m] for m in range(MB)]
    token = lax.broadcasted_iota(jnp.int32, (SLOT, ROWS), 1)
    slot_row = token % MB_TOK
    for m in range(MB):
        rank = jnp.int32(0)
        for before in range(m):
            rank = rank + jnp.where(names[before] == names[m], 1, 0)
        slot_row += jnp.where(token // MB_TOK == m, (names[m] * 2 + rank) * MB_TOK, 0)
    row = lax.broadcasted_iota(jnp.int32, (SLOT, ROWS), 0)
    for i, (dz, dy) in enumerate(MATES + [(0, 0)]):
        peer = chip((z + dz) % 2, (y + dy) % 4) * 2 + c
        chosen[i * SLOT : (i + 1) * SLOT] = jnp.where(
            slot_row == row + peer * SLOT, 1.0, 0.0
        ).astype(BF16)

    load_wd.wait()
    mul_1(0, 0)
    ag_halves(1, 0)
    ag_across(0, 0)
    ag_across(1, 0)
    ag_halves(0, 1)
    ag_halves(1, 1)
    ag_across(0, 1)
    ag_across(1, 1)
    mul_1(1, 0)
    mul_1(0, 1)
    ag_third(0, 0)
    mul_1(1, 1)
    ag_third(1, 0)
    mul_2(0, 0)
    mul_2(1, 0)
    ag_fourth(0, 0)
    mul_3(0, 0)
    ag_fourth(1, 0)
    ag_third(0, 1)
    mul_3(1, 0)
    row_sums(0)
    ag_third(1, 1)
    rs_first(0)
    spread_sums(0)
    mul_2(0, 1)
    ag_fourth(0, 1)
    mul_2(1, 1)
    mul_3(0, 1)
    rs_second(0)
    ag_fourth(1, 1)
    mul_3(1, 1)
    row_sums(1)
    rs_third(0)
    rs_first(1)
    spread_sums(1)
    rs_second(1)
    finish(0, totals_of(0))

    rs_third(1)
    for j in range(3):
        move_second(0, j)
    totals = totals_of(1)
    for j in range(3):
        routed[:, starts[j] : starts[j] + 2 * WIDTHS[j]] = place_rows(0, j)
    finish(1, totals, 0)
    move_second(1, 0)
    move_second(1, 1)
    put_part(0)
    move_second(1, 2)
    put_part(1)
    put_part(2)
    for k in range(4):
        grad_up(k)
    for j in range(3):
        wait_part(j)
    returned_ref[...] = landed[...]

    for h in range(2):

        @pl.loop(0, CHIPS)
        def _(k):
            sib_copy(h, k).wait_send()

        @pl.when(s > 0)
        def _():
            for j in range(3):
                move_copy(h, j).wait_send()

    for copy in sends:
        copy.wait_send()


def both(make):
    return tuple(make(t) for t in TOKS)


def layer(acts, grad_out, gain, live, senders, w_up, w_down):
    vmem, anyspace = pl.BlockSpec(memory_space=pltpu.VMEM), pl.BlockSpec(memory_space=pl.ANY)
    smem = pl.BlockSpec(memory_space=pltpu.SMEM)
    dma = pltpu.SemaphoreType.DMA
    return pl.pallas_call(
        layer_kernel,
        out_shape=[
            pltpu.VMEM((D, CHIP), BF16),
            pltpu.VMEM((SLOT, D), BF16),
        ],
        in_specs=[anyspace, anyspace, vmem, smem, smem, anyspace, anyspace],
        out_specs=[vmem, vmem],
        scratch_shapes=[
            pltpu.VMEM((D, CHIP), BF16),
            pltpu.VMEM((CHIP, D), BF16),
            both(lambda t: pltpu.VMEM((D, t), BF16)),
            both(lambda t: pltpu.VMEM((D, t), BF16)),
            both(lambda t: pltpu.VMEM((CHIP, t), F32)),
            both(lambda t: pltpu.VMEM((CHIP, t), F32)),
            both(lambda t: pltpu.VMEM((CHIP, t), BF16)),
            both(lambda t: pltpu.VMEM((D, t), BF16)),
            both(lambda t: pltpu.VMEM((CHIPS, LOCAL, t), BF16)),
            both(lambda t: pltpu.VMEM((LOCAL, t), BF16)),
            both(lambda t: pltpu.VMEM((2, LOCAL, t), BF16)),
            both(lambda t: pltpu.VMEM((2, LOCAL, t), BF16)),
            both(lambda t: pltpu.VMEM((2, LOCAL, t), BF16)),
            both(lambda t: pltpu.VMEM((LOCAL, t), BF16)),
            both(lambda t: pltpu.VMEM((2, LOCAL, t), BF16)),
            pltpu.VMEM((LOCAL, ROWS), BF16),
            pltpu.VMEM((LOCAL, ROWS), BF16),
            pltpu.VMEM((LOCAL, ROWS), F32),
            pltpu.VMEM((CHIPS, 8, 256), F32),
            pltpu.VMEM((8, 256), F32),
            pltpu.VMEM((8, 256), F32),
            both(lambda t: pltpu.VMEM((8, t), F32)),
            both(lambda t: pltpu.VMEM((8, t), F32)),
            both(lambda t: pltpu.VMEM((CHIPS, 8, t), F32)),
            pltpu.VMEM((16, CHIP), BF16),
            pltpu.VMEM((LOCAL, 128), F32),
            both(lambda t: pltpu.VMEM((LOCAL, t), BF16)),
            both(lambda t: pltpu.VMEM((CHIP, t), BF16)),
            pltpu.VMEM((CHIPS * SLOT, ROWS), BF16),
            pltpu.VMEM((CHIPS * SLOT, CHIP), F32),
            tuple(pltpu.VMEM((CHIPS * SLOT, 2 * w), BF16) for w in WIDTHS),
            pltpu.VMEM((SLOT, D), BF16),
            dma((4, N_AG)),
            dma((4, N_AG)),
            dma((8,)),
            dma((8,)),
            dma((2, 8)),
            dma((2, 8)),
            dma((2, CHIPS)),
            dma((2, CHIPS)),
            dma((4 * N_RS,)),
            dma((4 * N_RS,)),
            dma((2, 6)),
            dma((2, 6)),
            dma((7, 6)),
            dma((7, 6)),
            dma((4,)),
        ],
        compiler_params=pltpu.CompilerParams(
            collective_id=0, has_side_effects=True, vmem_limit_bytes=50 * MIB
        ),
        cost_estimate=pl.CostEstimate(
            flops=8 * ROWS * D * CHIP, bytes_accessed=20 * MIB, transcendentals=2 * ROWS * CHIP
        ),
    )(acts, grad_out, gain, live, senders, w_up, w_down)


def body(acts, grad_out, gain, w_up, w_down, senders, live):
    grad_up, returned = layer(acts.T, grad_out.T, gain, live, senders[:, 0], w_up, w_down)
    return (grad_up[None], returned)


def solution(mesh):
    in_specs = (
        P("section", "peer"),
        P("section", "peer"),
        P("section", "peer"),
        P("section", None, "peer"),
        P("section", "peer", None),
        P(),
        P("section"),
    )
    out_specs = (P("section", None, "peer"), P(("section", "peer"), None))
    return jax.shard_map(body, mesh=mesh, in_specs=in_specs, out_specs=out_specs, check_vma=False)
```

```python
import jax
import jax.numpy as jnp
from jax import lax
from jax.experimental import pallas as pl
from jax.experimental.pallas import tpu as pltpu
from jax.sharding import PartitionSpec as P

MESH = pl.DeviceIdType.MESH
F32 = jnp.float32
BF16 = jnp.bfloat16
MB = 16
MB_TOK = 32
ROWS = 512
TOKS = (256, 256)
FROM = (0, 256)
D = 5120
CHIP = 640
LOCAL = 320
PART = 160
CHIPS = 8
SLOT = 2 * MB_TOK
PIECE = 48
HEAD, TAIL = (0, PART), (PART, PART)
FIRST, BUT_FIRST = (0, PIECE), (PIECE, LOCAL - PIECE)
LAST, BUT_LAST = (LOCAL - PIECE, PIECE), (0, LOCAL - PIECE)
PARTS = (((LOCAL, 16),), ((LOCAL, 16),))
WIDTHS = (128, 128, 64)
GU = 1280
MIB = 2**20

MATES = [(0, 1), (0, 2), (0, 3), (1, 0), (1, 1), (1, 2), (1, 3)]
SUM_ORDER = [(1, 2), (1, 1), (1, 3), (0, 1), (0, 3), (0, 2), (1, 0), (0, 0)]
LAG = 3
N_AG = 21
N_RS = 12


def nn_dot(a, b):
    return jnp.dot(a, b, preferred_element_type=F32)


def nt_dot(a, b):
    return lax.dot_general(a, b, (((1,), (1,)), ((), ())), preferred_element_type=F32)


def tn_dot(a, b):
    return lax.dot_general(a, b, (((0,), (0,)), ((), ())), preferred_element_type=F32)


def span(h):
    return slice(FROM[h], FROM[h] + TOKS[h])


def pick(table, k):
    out = table[0]
    for i in range(1, len(table)):
        out = jnp.where(k == i, table[i], out)
    return out


def layer_kernel(
    acts_hbm, grad_hbm, gain_ref, live_ref, senders_ref, wu_hbm, wd_hbm,
    gu_ref, returned_ref,
    wu, wd, g_all, x_all, pre, bh, bp, part, sib_part, r_a, r_b, r_c, r_e, r_d, r_p,
    acts, grads, normed, facts, my_facts, sib_facts, sums, sib_sums, all_sums, weight_rows,
    gain_rows, out_buf, moved, chosen, routed, stage, landed,
    ag_send, ag_recv, facts_send, facts_recv, sums_send, sums_recv,
    sib_send, sib_recv, rs_send, rs_recv, move_send, move_recv, put_send, put_recv,
    local_sem,
):
    s, p = lax.axis_index("section"), lax.axis_index("peer")
    q_me, c = p // 2, p % 2
    z, y, oc = q_me // 4, q_me % 4, 1 - c
    z2, yp, ym, y2 = 1 - z, (y + 1) % 4, (y + 3) % 4, (y + 2) % 4
    sections = lax.axis_size("section")

    def dev(zz, yy, cc):
        return (s, (zz * 4 + yy) * 2 + cc)

    def mate(i):
        dz, dy = MATES[i]
        return dev((z + dz) % 2, (y + dy) % 4, c)

    def mate_from(i):
        dz, dy = MATES[i]
        return ((z + dz) % 2) * 4 + (y + 4 - dy) % 4

    sibling = dev(z, y, oc)
    sends = []

    def remote(src, dst, ssem, rsem, where):
        return pltpu.make_async_remote_copy(
            src_ref=src, dst_ref=dst, send_sem=ssem, recv_sem=rsem,
            device_id=where, device_id_type=MESH,
        )

    def send(src, dst, ssem, rsem, where):
        copy = remote(src, dst, ssem, rsem, where)
        copy.start()
        sends.append(copy)

    def recv(dst, ssem, rsem):
        remote(dst, dst, ssem, rsem, sibling).wait_recv()

    def rows(at, count):
        return pl.ds(pl.multiple_of(at, 16), count)

    load_grad = pltpu.make_async_copy(grad_hbm, grads, local_sem.at[0])
    load_acts = pltpu.make_async_copy(acts_hbm, acts, local_sem.at[1])
    load_wd = pltpu.make_async_copy(wd_hbm.at[0], wd, local_sem.at[2])
    load_wu = pltpu.make_async_copy(wu_hbm.at[0], wu, local_sem.at[3])
    load_grad.start()
    load_acts.start()
    load_wd.start()
    load_wu.start()

    barrier = pltpu.get_barrier_semaphore()
    pl.semaphore_signal(barrier, inc=1, device_id=sibling, device_id_type=MESH)
    for i in range(7):
        pl.semaphore_signal(barrier, inc=1, device_id=mate(i), device_id_type=MESH)
    for step in (1, sections - 1):
        pl.semaphore_signal(
            barrier, inc=1, device_id=((s + step) % sections, p), device_id_type=MESH
        )
    pl.semaphore_wait(barrier, 10)

    bufs = (g_all, x_all)

    def block(a, h, zz, yy, cc, half=None):
        at = (zz * 4 + yy) * CHIP + cc * LOCAL
        first, count = (0, LOCAL) if half is None else half
        return bufs[a][h].at[rows(at + first, count)]

    def ag_start(a, h, tag, zz, yy, where, half=None):
        ref = block(a, h, zz, yy, c, half)
        send(ref, ref, ag_send.at[2 * a + h, tag], ag_recv.at[2 * a + h, tag], where)

    def ag_wait(a, h, tag, zz, yy, cc, half=None):
        recv(block(a, h, zz, yy, cc, half), ag_send.at[2 * a + h, tag], ag_recv.at[2 * a + h, tag])

    def ag_own(a, h):
        ag_start(a, h, 0, z, y, dev(z2, y, c))
        ag_start(a, h, 1, z, y, dev(z, yp, c))
        ag_start(a, h, 2, z, y, dev(z, ym, c))
        ag_start(a, h, 9, z, y, sibling)

    def ag_halves(a, h):
        ag_wait(a, h, 1, z, ym, c)
        ag_start(a, h, 3, z, ym, dev(z, yp, c), HEAD)
        ag_wait(a, h, 2, z, yp, c)
        ag_start(a, h, 4, z, yp, dev(z, ym, c), TAIL)
        ag_start(a, h, 19, z, yp, dev(z2, y, c), FIRST)
        ag_start(a, h, 20, z, ym, dev(z2, y, c), LAST)
        ag_start(a, h, 10, z, ym, sibling)
        ag_start(a, h, 11, z, yp, sibling)

    def ag_across(a, h):
        ag_wait(a, h, 0, z2, y, c)
        ag_start(a, h, 5, z2, y, dev(z, yp, c), BUT_LAST)
        ag_start(a, h, 6, z2, y, dev(z, ym, c), BUT_FIRST)
        ag_start(a, h, 12, z2, y, sibling)

    def ag_third(a, h):
        ag_wait(a, h, 3, z, y2, c, HEAD)
        ag_start(a, h, 7, z, y2, dev(z2, y, c), HEAD)
        ag_wait(a, h, 4, z, y2, c, TAIL)
        ag_start(a, h, 8, z, y2, dev(z2, y, c), TAIL)
        ag_start(a, h, 13, z, y2, sibling, HEAD)
        ag_start(a, h, 14, z, y2, sibling, TAIL)

    def ag_fourth(a, h):
        ag_wait(a, h, 5, z2, ym, c, BUT_LAST)
        ag_wait(a, h, 20, z2, ym, c, LAST)
        ag_start(a, h, 15, z2, ym, sibling)
        ag_wait(a, h, 6, z2, yp, c, BUT_FIRST)
        ag_wait(a, h, 19, z2, yp, c, FIRST)
        ag_start(a, h, 16, z2, yp, sibling)
        ag_wait(a, h, 7, z2, y2, c, HEAD)
        ag_start(a, h, 17, z2, y2, sibling, HEAD)
        ag_wait(a, h, 8, z2, y2, c, TAIL)
        ag_start(a, h, 18, z2, y2, sibling, TAIL)

    def multiply(a, h, pair, first=False):
        at = pair * (2 * CHIP)
        at = pl.ds(pl.multiple_of(at, 2 * CHIP), 2 * CHIP)
        if a == 0:
            total, term = bh, nn_dot(wd[:, at], g_all[h][at])
        else:
            total, term = pre, tn_dot(wu[at], x_all[h][at])
        total[h][...] = term if first else total[h][...] + term

    here, across = z * 2 + y // 2, z2 * 2 + y // 2
    here_2, across_2 = z * 2 + 1 - y // 2, z2 * 2 + 1 - y // 2

    def mul_1(a, h):
        ag_wait(a, h, 9, z, y, oc)
        ag_wait(a, h, 10, z, ym, oc)
        ag_wait(a, h, 11, z, yp, oc)
        multiply(a, h, here, True)

    def mul_2(a, h):
        ag_wait(a, h, 13, z, y2, oc, HEAD)
        ag_wait(a, h, 14, z, y2, oc, TAIL)
        multiply(a, h, here_2)

    def mul_3(a, h):
        ag_wait(a, h, 12, z2, y, oc)
        ag_wait(a, h, 15, z2, ym, oc)
        ag_wait(a, h, 16, z2, yp, oc)
        multiply(a, h, across)
        ag_wait(a, h, 17, z2, y2, oc, HEAD)
        ag_wait(a, h, 18, z2, y2, oc, TAIL)
        multiply(a, h, across_2)

    def put_row(ref, at, row):
        ref[at : at + 1] = row[:, 0:256]
        ref[at + 1 : at + 2, 0 : row.shape[1] - 256] = row[:, 256:]

    def get_row(ref, at, count):
        return jnp.concatenate([ref[at : at + 1], ref[at + 1 : at + 2, 0 : count - 256]], axis=1)

    own = rows(q_me * CHIP + c * LOCAL, LOCAL)
    load_grad.wait()
    for h in range(2):
        token = lax.broadcasted_iota(jnp.int32, (LOCAL, TOKS[h]), 1) + FROM[h]
        alive = (token // MB_TOK < live_ref[0]).astype(F32)
        g_all[h][own] = (grads[:, span(h)].astype(F32) * alive).astype(BF16)
    ag_own(0, 0)
    load_acts.wait()
    values = acts[...].astype(F32)
    mean_here = jnp.mean(values, axis=0, keepdims=True)
    spread = values - mean_here
    put_row(my_facts, 0, mean_here)
    put_row(my_facts, 2, jnp.sum(spread * spread, axis=0, keepdims=True))
    gain_row = gain_ref[...].astype(F32)
    put_row(my_facts, 4, gain_row)
    send(my_facts, sib_facts, facts_send.at[7], facts_recv.at[7], sibling)
    recv(sib_facts, facts_send.at[7], facts_recv.at[7])
    mean_a, mean_b = my_facts[0:2], sib_facts[0:2]
    mean_chip = 0.5 * (mean_a + mean_b)
    apart_a, apart_b = mean_a - mean_chip, mean_b - mean_chip
    facts[q_me, 0:2] = mean_chip
    facts[q_me, 2:4] = (
        my_facts[2:4] + sib_facts[2:4] + LOCAL * (apart_a * apart_a + apart_b * apart_b)
    )
    facts[q_me, 4:6] = jnp.where(c == 0, my_facts[4:6], sib_facts[4:6])
    facts[q_me, 6:8] = jnp.where(c == 0, sib_facts[4:6], my_facts[4:6])
    for i in range(7):
        send(facts.at[q_me], facts.at[q_me], facts_send.at[i], facts_recv.at[i], mate(i))
    ag_own(0, 1)
    across_eye = lax.broadcasted_iota(jnp.int32, (LOCAL, LOCAL), 0) == lax.broadcasted_iota(
        jnp.int32, (LOCAL, LOCAL), 1
    )
    gain_col = jnp.sum(jnp.where(across_eye, gain_row, 0.0), axis=1, keepdims=True)
    gain_rows[...] = jnp.broadcast_to(gain_col, (LOCAL, 128))
    for i in range(7):
        recv(facts.at[mate_from(i)], facts_send.at[i], facts_recv.at[i])
    means = [facts[i, 0:2] for i in range(CHIPS)]
    mean_two = sum(means) / CHIPS
    square_two = sum(facts[i, 2:4] for i in range(CHIPS))
    square_two += CHIP * sum((m - mean_two) * (m - mean_two) for m in means)
    rstd_two = lax.rsqrt(square_two / D + 1e-05)
    mean_row = jnp.concatenate([mean_two[0:1], mean_two[1:2]], axis=1)
    rstd_row = jnp.concatenate([rstd_two[0:1], rstd_two[1:2]], axis=1)
    normed[...] = (acts[...].astype(F32) - mean_row) * rstd_row
    for h in range(2):
        x_all[h][own] = (normed[:, span(h)] * gain_col).astype(BF16)
        ag_own(1, h)

    def row_sums(h):
        def tile(i, second):
            at = rows(i * 128, 128)
            u = pre[h][at]
            slope = (
                0.5 * (1.0 + lax.erf(u * 0.7071067811865476))
                + u * jnp.exp(-0.5 * u * u) * 0.3989422804014327
            )
            b = (bh[h][at] * slope).astype(BF16)
            bp[h][at] = b
            return second + jnp.sum(b.astype(F32) * u, axis=0, keepdims=True)

        second = lax.fori_loop(0, CHIP // 128, tile, jnp.zeros((1, TOKS[h]), F32))
        first = nn_dot(weight_rows[...], bp[h][...])
        sums[h][0:1] = first[0:1] + first[1:2]
        sums[h][1:2] = second
        send(sums[h], sib_sums[h], sums_send.at[h, 7], sums_recv.at[h, 7], sibling)

    def spread_sums(h):
        recv(sib_sums[h], sums_send.at[h, 7], sums_recv.at[h, 7])
        all_sums[h][q_me] = sums[h][...] + sib_sums[h][...]
        mine = all_sums[h].at[q_me]
        for i in range(7):
            send(mine, mine, sums_send.at[h, i], sums_recv.at[h, i], mate(i))

    def chip(zz, yy):
        return zz * 4 + yy

    def offset(j):
        return (c * 192, 128 - c * 64, (1 - c) * 256)[j]

    def part_rows(h, j):
        count, over = PARTS[h][j]
        first = offset(j) if len(PARTS[h]) > 1 else 0
        half = count // 2
        return dict(
            all=(first, count),
            head=(first, half),
            tail=(first + half, half),
            first=(first, over),
            but_first=(first + over, count - over),
            last=(first + count - over, over),
            but_last=(first, count - over),
        )

    def mine_of(h, q, at):
        first, count = at
        return part[h].at[rows(q * CHIP + c * LOCAL + first, count)]

    def cut(ref, at):
        first, count = at
        return ref.at[rows(first, count)]

    q_p, q_m, q_2 = chip(z, yp), chip(z, ym), chip(z, y2)
    q_z, q_zp, q_zm, q_z2 = chip(z2, y), chip(z2, yp), chip(z2, ym), chip(z2, y2)

    def sib_copy(h, q):
        return remote(
            part[h].at[rows(q * CHIP + oc * LOCAL, LOCAL)], sib_part[h].at[q],
            sib_send.at[h, q], sib_recv.at[h, q], sibling,
        )

    def rs_copy(h, tag, src, dst, where):
        return remote(src, dst, rs_send.at[tag], rs_recv.at[tag], where)

    def rs_start(h, tag, src, dst, where):
        copy = rs_copy(h, tag, src, dst, where)
        copy.start()
        sends.append(copy)

    def rs_wait(h, tag, dst):
        recv(dst, rs_send.at[tag], rs_recv.at[tag])

    def add(ref, *others):
        total = ref[...].astype(F32)
        for other in others:
            total += other[...].astype(F32)
        ref[...] = total.astype(BF16)

    def tags(h, j):
        return (h * len(PARTS[0]) + j) * N_RS

    def rs_first(h):
        across, up, down = dev(z2, y, c), dev(z, yp, c), dev(z, ym, c)

        def puts(j):
            t, at = tags(h, j), part_rows(h, j)

            def put(tag, q, where, dst, to):
                return lambda: rs_copy(h, t + tag, mine_of(h, q, at[where]), cut(dst, at[where]), to)

            return [
                [put(0, q_z2, "all", r_a[h], across)],
                [
                    put(1, q_zp, "but_first", r_b[h].at[0], up),
                    put(10, q_zp, "first", r_p[h].at[0], across),
                ],
                [
                    put(2, q_zm, "but_last", r_b[h].at[1], down),
                    put(11, q_zm, "last", r_p[h].at[1], across),
                ],
                [put(3, q_p, "tail", r_e[h].at[0], up)],
                [put(4, q_m, "head", r_e[h].at[1], down)],
            ]

        early = [puts(j) for j in range(len(PARTS[h]))]

        def chip_at(k):
            dz = pick([t[0] for t in SUM_ORDER], k)
            dy = pick([t[1] for t in SUM_ORDER], k)
            return chip((z + dz) % 2, (y + dy) % 4)

        def product(k):
            q = chip_at(k)
            at = pl.ds(pl.multiple_of(q * CHIP, CHIP), CHIP)
            part[h][at] = nn_dot(wu[at], bp[h][...]).astype(BF16)
            sib_copy(h, q).start()

        def join(k):
            q = chip_at(k)
            sib_copy(h, q).wait_recv()
            add(mine_of(h, q, (0, LOCAL)), sib_part[h].at[q])

        @pl.loop(0, LAG)
        def _(k):
            product(k)

        @pl.loop(LAG, CHIPS)
        def _(k):
            product(k)
            join(k - LAG)
            for i, makes in enumerate(early[0]):

                @pl.when(k == LAG + i)
                def _(makes=makes):
                    for make in makes:
                        make().start()

        @pl.loop(CHIPS - LAG, CHIPS)
        def _(k):
            join(k)

        for j, groups in enumerate(early):
            for make in [m for group in groups for m in group]:
                copy = make()
                if j > 0:
                    copy.start()
                sends.append(copy)

    def rs_second(h, j=0):
        t, at = tags(h, j), part_rows(h, j)
        rs_wait(h, t, cut(r_a[h], at["all"]))
        add(mine_of(h, q_2, at["all"]), cut(r_a[h], at["all"]))
        head, tail = at["head"], at["tail"]
        rs_start(h, t + 5, mine_of(h, q_2, head), cut(r_c[h].at[0], head), dev(z, yp, c))
        rs_start(h, t + 6, mine_of(h, q_2, tail), cut(r_c[h].at[1], tail), dev(z, ym, c))
        from_m, from_p = cut(r_b[h].at[0], at["but_first"]), cut(r_b[h].at[1], at["but_last"])
        rs_wait(h, t + 1, from_m)
        rs_wait(h, t + 2, from_p)
        add(mine_of(h, q_z, at["but_first"]), from_m)
        add(mine_of(h, q_z, at["but_last"]), from_p)
        rs_start(
            h, t + 7, mine_of(h, q_z, at["all"]), cut(r_d[h], at["all"]), dev(z2, y, c)
        )
        for tag, q, i, where in ((10, q_p, 0, "first"), (11, q_m, 1, "last")):
            there = cut(r_p[h].at[i], at[where])
            rs_wait(h, t + tag, there)
            add(mine_of(h, q, at[where]), there)

    def rs_third(h, j=0):
        t, at = tags(h, j), part_rows(h, j)
        for tag, q, i, where, to in (
            (0, q_p, 0, "head", dev(z, yp, c)),
            (1, q_m, 1, "tail", dev(z, ym, c)),
        ):
            there = cut(r_c[h].at[i], at[where])
            rs_wait(h, t + 5 + tag, there)
            add(mine_of(h, q, at[where]), there)
            rs_start(h, t + 8 + tag, mine_of(h, q, at[where]), cut(r_e[h].at[i], at[where]), to)

    starts = [2 * sum(WIDTHS[:j]) for j in range(3)]

    def place_of(h, j, core):
        return moved[h].at[rows(starts[j] + core * WIDTHS[j], WIDTHS[j])]

    def move_copy(h, j):
        return remote(
            out_buf[h].at[rows(offset(j), WIDTHS[j])], place_of(h, j, c), move_send.at[h, j],
            move_recv.at[h, j], ((s + sections - 1) % sections, p),
        )

    def totals_of(h):
        for i in range(7):
            recv(all_sums[h].at[mate_from(i)], sums_send.at[h, i], sums_recv.at[h, i])
        return sum(all_sums[h][i] for i in range(CHIPS)) / D

    def finish(h, totals, j=0):
        t, at = tags(h, j), part_rows(h, j)
        mine = at["all"]
        rs_wait(h, t + 7, cut(r_d[h], mine))
        rs_wait(h, t + 3, cut(r_e[h].at[0], at["tail"]))
        rs_wait(h, t + 4, cut(r_e[h].at[1], at["head"]))
        rs_wait(h, t + 8, cut(r_e[h].at[0], at["head"]))
        rs_wait(h, t + 9, cut(r_e[h].at[1], at["tail"]))
        summed = mine_of(h, q_me, mine)[...].astype(F32)
        for ref in (r_d[h], r_e[h].at[0], r_e[h].at[1]):
            summed += cut(ref, mine)[...].astype(F32)
        here = rows(*mine)
        gain_here = gain_rows[here, 0:1]
        back = summed * gain_here - totals[0:1] - normed[here, span(h)] * totals[1:2]
        grad_here = g_all[h][rows(q_me * CHIP + c * LOCAL + mine[0], mine[1])].astype(F32)
        out_buf[h][here] = (rstd_row[:, span(h)] * back + grad_here).astype(BF16)

        @pl.when(s > 0)
        def _():
            for i in range(3) if len(PARTS[h]) == 1 else (j,):
                move_copy(h, i).start()

    def move_second(h, j):
        there = place_of(h, j, c)

        @pl.when(s < sections - 1)
        def _():
            recv(there, move_send.at[h, j], move_recv.at[h, j])

        @pl.when(s == sections - 1)
        def _():
            there[...] = jnp.zeros((WIDTHS[j], TOKS[h]), BF16)

        send(there, there, move_send.at[h, 3 + j], move_recv.at[h, 3 + j], sibling)

    def place_rows(h, j):
        recv(place_of(h, j, oc), move_send.at[h, 3 + j], move_recv.at[h, 3 + j])
        features = moved[h][starts[j] : starts[j] + 2 * WIDTHS[j]]
        return nt_dot(chosen[:, span(h)], features)

    COLUMNS = (((0, 128, 0), (512, 128, 128)), ((128, 128, 0), (384, 128, 128)), ((256, 128, 0),))

    def part_columns(q, at, width):
        return pl.ds(pl.multiple_of(q * CHIP + at, 128), width)

    def put_part(j):
        width = 2 * WIDTHS[j]
        both_phases = routed[:, starts[j] : starts[j] + width] + place_rows(1, j)
        stage[j][...] = both_phases.astype(BF16)
        for i in range(7):
            for n, (at, size, source) in enumerate(COLUMNS[j]):
                send(
                    stage[j].at[pl.ds(i * SLOT, SLOT), pl.ds(source, size)],
                    landed.at[:, part_columns(q_me, at, size)],
                    put_send.at[i, 2 * j + n], put_recv.at[i, 2 * j + n], mate(i),
                )
        for at, size, source in COLUMNS[j]:
            landed[:, part_columns(q_me, at, size)] = stage[j][7 * SLOT :, source : source + size]

    def wait_part(j):
        for i in range(7):
            for n, (at, size, _) in enumerate(COLUMNS[j]):
                there = landed.at[:, part_columns(mate_from(i), at, size)]
                recv(there, put_send.at[i, 2 * j + n], put_recv.at[i, 2 * j + n])

    count = live_ref[0].astype(F32)

    def grad_up(k):
        at = pl.ds(k * GU, GU)
        term = nt_dot(x_all[0][at], bp[0][...]) + nt_dot(x_all[1][at], bp[1][...])
        gu_ref[at] = (term / count).astype(BF16)

    ag_halves(0, 0)
    load_wu.wait()
    weights = jnp.zeros((16, CHIP), F32)
    for i in range(CHIPS):
        for j in range(2):
            gain_ij = get_row(facts.at[i], 4 + 2 * j, LOCAL)
            gain_ij = jnp.broadcast_to(gain_ij, (16, LOCAL)).astype(BF16)
            at = i * CHIP + j * LOCAL
            weights += nn_dot(gain_ij, wu[at : at + LOCAL])
    high = weights.astype(BF16).astype(F32)
    line = lax.broadcasted_iota(jnp.int32, (16, CHIP), 0)
    weight_rows[...] = jnp.where(
        line == 0, high, jnp.where(line == 1, weights - high, 0.0)
    ).astype(BF16)
    base = jnp.minimum(s + 1, sections - 1) * MB
    names = [senders_ref[base + m] for m in range(MB)]
    token = lax.broadcasted_iota(jnp.int32, (SLOT, ROWS), 1)
    slot_row = token % MB_TOK
    for m in range(MB):
        rank = jnp.int32(0)
        for before in range(m):
            rank = rank + jnp.where(names[before] == names[m], 1, 0)
        slot_row += jnp.where(token // MB_TOK == m, (names[m] * 2 + rank) * MB_TOK, 0)
    row = lax.broadcasted_iota(jnp.int32, (SLOT, ROWS), 0)
    for i, (dz, dy) in enumerate(MATES + [(0, 0)]):
        peer = chip((z + dz) % 2, (y + dy) % 4) * 2 + c
        chosen[i * SLOT : (i + 1) * SLOT] = jnp.where(
            slot_row == row + peer * SLOT, 1.0, 0.0
        ).astype(BF16)

    load_wd.wait()
    mul_1(0, 0)
    ag_halves(1, 0)
    ag_across(0, 0)
    ag_across(1, 0)
    ag_halves(0, 1)
    ag_halves(1, 1)
    ag_across(0, 1)
    ag_across(1, 1)
    mul_1(1, 0)
    ag_third(0, 0)
    mul_1(0, 1)
    ag_third(1, 0)
    mul_1(1, 1)
    mul_2(0, 0)
    mul_2(1, 0)
    ag_fourth(0, 0)
    mul_3(0, 0)
    ag_fourth(1, 0)
    ag_third(0, 1)
    mul_3(1, 0)
    row_sums(0)
    ag_third(1, 1)
    rs_first(0)
    spread_sums(0)
    mul_2(0, 1)
    ag_fourth(0, 1)
    mul_2(1, 1)
    mul_3(0, 1)
    rs_second(0)
    ag_fourth(1, 1)
    mul_3(1, 1)
    row_sums(1)
    rs_third(0)
    rs_first(1)
    spread_sums(1)
    rs_second(1)
    finish(0, totals_of(0))

    rs_third(1)
    for j in range(3):
        move_second(0, j)
    totals = totals_of(1)
    for j in range(3):
        routed[:, starts[j] : starts[j] + 2 * WIDTHS[j]] = place_rows(0, j)
    finish(1, totals, 0)
    move_second(1, 0)
    move_second(1, 1)
    put_part(0)
    move_second(1, 2)
    put_part(1)
    put_part(2)
    for k in range(4):
        grad_up(k)
    for j in range(3):
        wait_part(j)
    returned_ref[...] = landed[...]

    for h in range(2):

        @pl.loop(0, CHIPS)
        def _(k):
            sib_copy(h, k).wait_send()

        @pl.when(s > 0)
        def _():
            for j in range(3):
                move_copy(h, j).wait_send()

    for copy in sends:
        copy.wait_send()


def both(make):
    return tuple(make(t) for t in TOKS)


def layer(acts, grad_out, gain, live, senders, w_up, w_down):
    vmem, anyspace = pl.BlockSpec(memory_space=pltpu.VMEM), pl.BlockSpec(memory_space=pl.ANY)
    smem = pl.BlockSpec(memory_space=pltpu.SMEM)
    dma = pltpu.SemaphoreType.DMA
    return pl.pallas_call(
        layer_kernel,
        out_shape=[
            pltpu.VMEM((D, CHIP), BF16),
            pltpu.VMEM((SLOT, D), BF16),
        ],
        in_specs=[anyspace, anyspace, vmem, smem, smem, anyspace, anyspace],
        out_specs=[vmem, vmem],
        scratch_shapes=[
            pltpu.VMEM((D, CHIP), BF16),
            pltpu.VMEM((CHIP, D), BF16),
            both(lambda t: pltpu.VMEM((D, t), BF16)),
            both(lambda t: pltpu.VMEM((D, t), BF16)),
            both(lambda t: pltpu.VMEM((CHIP, t), F32)),
            both(lambda t: pltpu.VMEM((CHIP, t), F32)),
            both(lambda t: pltpu.VMEM((CHIP, t), BF16)),
            both(lambda t: pltpu.VMEM((D, t), BF16)),
            both(lambda t: pltpu.VMEM((CHIPS, LOCAL, t), BF16)),
            both(lambda t: pltpu.VMEM((LOCAL, t), BF16)),
            both(lambda t: pltpu.VMEM((2, LOCAL, t), BF16)),
            both(lambda t: pltpu.VMEM((2, LOCAL, t), BF16)),
            both(lambda t: pltpu.VMEM((2, LOCAL, t), BF16)),
            both(lambda t: pltpu.VMEM((LOCAL, t), BF16)),
            both(lambda t: pltpu.VMEM((2, LOCAL, t), BF16)),
            pltpu.VMEM((LOCAL, ROWS), BF16),
            pltpu.VMEM((LOCAL, ROWS), BF16),
            pltpu.VMEM((LOCAL, ROWS), F32),
            pltpu.VMEM((CHIPS, 8, 256), F32),
            pltpu.VMEM((8, 256), F32),
            pltpu.VMEM((8, 256), F32),
            both(lambda t: pltpu.VMEM((8, t), F32)),
            both(lambda t: pltpu.VMEM((8, t), F32)),
            both(lambda t: pltpu.VMEM((CHIPS, 8, t), F32)),
            pltpu.VMEM((16, CHIP), BF16),
            pltpu.VMEM((LOCAL, 128), F32),
            both(lambda t: pltpu.VMEM((LOCAL, t), BF16)),
            both(lambda t: pltpu.VMEM((CHIP, t), BF16)),
            pltpu.VMEM((CHIPS * SLOT, ROWS), BF16),
            pltpu.VMEM((CHIPS * SLOT, CHIP), F32),
            tuple(pltpu.VMEM((CHIPS * SLOT, 2 * w), BF16) for w in WIDTHS),
            pltpu.VMEM((SLOT, D), BF16),
            dma((4, N_AG)),
            dma((4, N_AG)),
            dma((8,)),
            dma((8,)),
            dma((2, 8)),
            dma((2, 8)),
            dma((2, CHIPS)),
            dma((2, CHIPS)),
            dma((4 * N_RS,)),
            dma((4 * N_RS,)),
            dma((2, 6)),
            dma((2, 6)),
            dma((7, 6)),
            dma((7, 6)),
            dma((4,)),
        ],
        compiler_params=pltpu.CompilerParams(
            collective_id=0, has_side_effects=True, vmem_limit_bytes=50 * MIB
        ),
        cost_estimate=pl.CostEstimate(
            flops=8 * ROWS * D * CHIP, bytes_accessed=20 * MIB, transcendentals=2 * ROWS * CHIP
        ),
    )(acts, grad_out, gain, live, senders, w_up, w_down)


def body(acts, grad_out, gain, w_up, w_down, senders, live):
    grad_up, returned = layer(acts.T, grad_out.T, gain, live, senders[:, 0], w_up, w_down)
    return (grad_up[None], returned)


def solution(mesh):
    in_specs = (
        P("section", "peer"),
        P("section", "peer"),
        P("section", "peer"),
        P("section", None, "peer"),
        P("section", "peer", None),
        P(),
        P("section"),
    )
    out_specs = (P("section", None, "peer"), P(("section", "peer"), None))
    return jax.shard_map(body, mesh=mesh, in_specs=in_specs, out_specs=out_specs, check_vma=False)
```
